256 devices in a mesh: dp: 64 (over z, x, core), tensor: 4 (over y).
Axes of the slice: x: 4, y: 4, z: 8, core: 2. Of those that a mesh axis runs over, the one named last changes fastest.
Arguments:
- grads: bfloat16 [2, 64, 128, 12800], P(None, 'dp', None, 'tensor'), may hold values from -16 to 16, as said below
- errors: float32 [2, 64, 128, 12800], P(None, 'dp', None, 'tensor'), may hold values from -4 to 4
- q_prev: float32 [2, 32, 12800], P(None, None, 'tensor'), may hold values from -0.0546875 to 0.0546875
Outputs:
- rebuilt: bfloat16 [2, 128, 12800], P(None, None, 'tensor')
- new_errors: float32 [2, 64, 128, 12800], P(None, 'dp', None, 'tensor')
- new_q: float32 [2, 32, 12800], P(None, None, 'tensor')
The draws below stay inside these ranges and needn't reach their ends.
Inputs may be any that keep to these rules, and one draw needn't show every extreme that they name: `grads`: each replica's gradient.
All inputs are finite; a program needn't handle non-finite values.
Results may differ from the reference program's by a relative error of at most 0.001.
Values sent between devices are 32-bit elements; how exact they have to be, the bound alone decides.
No kernel may reach another device: no remote copies, remote signals or barrier semaphores. Data moves between devices by JAX's collectives and lax.ppermute only.
A program may use at most 64 MiB of HBM per device.

```python
import jax
import jax.numpy as jnp
from jax import lax

FF = 12800
RANK = 32
ROWS = 128
N_DP = 64


def draw_grads(key, part):
    key = jax.random.fold_in(key, 11)
    key_scale, key_shared, key_noise = jax.random.split(key, 3)
    row_scale = jnp.exp(jax.random.uniform(key_scale, (2, 1, ROWS, 1), jnp.float32, 0.0, jnp.log(3.0)))
    shared = jnp.clip(jax.random.normal(key_shared, (2, 1, ROWS, FF), jnp.float32), -4.0, 4.0)
    noise = jnp.clip(jax.random.normal(key_noise, (2, N_DP, ROWS, FF), jnp.float32), -4.0, 4.0)
    return (row_scale * shared + noise).astype(jnp.bfloat16)


def block_scale(stream_key, extent, pieces, least, top_value):
    def one(dim, blocks):
        heights = jax.random.uniform(jax.random.fold_in(jax.random.fold_in(stream_key, 6), dim), (blocks,), jnp.float32, least / len(pieces), top_value / len(pieces))
        return jnp.repeat(jnp.exp(heights), extent[dim] // blocks).reshape((-1,) + (1,) * (len(extent) - dim - 1))

    level = one(*pieces[0])
    for cut in pieces[1:]:
        level = level * one(*cut)
    return level


def scatter_about(stream_key, dims, deviation, limit, cuts=(), held_as=jnp.bfloat16):
    result = deviation * jax.random.normal(stream_key, dims, jnp.float32)
    if cuts:
        result = result * block_scale(stream_key, dims, cuts, -0.22, 0.18)
    return jnp.clip(result, -limit, limit).astype(held_as)


def setup_inputs(seed: int = 0) -> dict:
    key_list = jax.random.split(jax.random.key(seed), 4)
    grads = draw_grads(jax.random.fold_in(key_list[3], 71), 0)
    errors = scatter_about(key_list[1], (2, N_DP, ROWS, FF), 0.5, 4.0, ((1, 64), (3, 4)), jnp.float32)
    q_prev = scatter_about(key_list[2], (2, RANK, FF), FF ** -0.5, 0.0546875, ((2, 4),), jnp.float32)
    return {"grads": grads, "errors": errors, "q_prev": q_prev}


def compress(corrected, q_prev):
    hi = lax.Precision.HIGHEST
    left = jnp.einsum('irf,kf->rk', corrected, q_prev, precision=hi)
    gram = jnp.dot(left.T, left, precision=hi)
    chol = jnp.linalg.cholesky(gram)
    ortho = jax.scipy.linalg.solve_triangular(chol, left.T, lower=True).T
    new_q = jnp.einsum('irf,rk->kf', corrected, ortho, precision=hi) / N_DP
    approx = jnp.dot(ortho, new_q, precision=hi)
    return (approx.astype(jnp.bfloat16), corrected - approx[None], new_q)

def reference(grads, errors, q_prev):
    rebuilt_list, error_list, q_list = ([], [], [])
    for index in range(2):
        corrected = grads[index].astype(jnp.float32) + errors[index]
        rebuilt_one, error_one, q_one = compress(corrected, q_prev[index])
        rebuilt_list.append(rebuilt_one)
        error_list.append(error_one)
        q_list.append(q_one)
    return (jnp.stack(rebuilt_list), jnp.stack(error_list), jnp.stack(q_list))
```

```python
import jax
import jax.numpy as jnp
from jax import lax
from jax.experimental import pallas as pl
from jax.experimental.pallas import tpu as pltpu
from jax.sharding import Mesh
from jax.sharding import PartitionSpec as P

F32 = jnp.float32
BF16 = jnp.bfloat16
SIZES = {"z": 8, "x": 4, "core": 2, "tensor": 4}
RANK = 32
ROWS = 128
COLS = 3200
TILE = 640
VMEM_BYTES = 24 * 1024 * 1024


def params():
    return pltpu.CompilerParams(vmem_limit_bytes=VMEM_BYTES)


def split(value):
    high = value.astype(BF16)
    return high, (value - high.astype(F32)).astype(BF16)


def matmul(a, b, dims):
    return lax.dot_general(a, b, (dims, ((), ())), preferred_element_type=F32)


def correct_kernel(core_ref, g_own, g_oth, e_own, e_oth, q_own, q_oth, c_own, c_oth, left_own, left_oth):
    step = pl.program_id(0)
    for g, e, q, c_out, left in (
        (g_oth, e_oth, q_oth, c_oth, left_oth),
        (g_own, e_own, q_own, c_own, left_own),
    ):
        c = g[0, 0].astype(F32) + e[0, 0]
        c_out[...] = c
        c_hi, c_lo = split(c)
        q_hi, q_lo = split(q[0])
        both = matmul(jnp.concatenate([q_hi, q_lo], axis=0), c_hi, ((1,), (1,)))
        part = both[:RANK] + both[RANK:] + matmul(q_hi, c_lo, ((1,), (1,)))
        before = jnp.where(step == 0, jnp.zeros_like(part), left[...])
        left[...] = before + part


def correct(core, grads, errors, q_prev):
    own = lambda j, s: (s[0], 0, 0, j)
    oth = lambda j, s: (1 - s[0], 0, 0, j)
    own3 = lambda j, s: (s[0], 0, j)
    oth3 = lambda j, s: (1 - s[0], 0, j)
    block = (1, 1, ROWS, TILE)
    grid_spec = pltpu.PrefetchScalarGridSpec(
        num_scalar_prefetch=1,
        grid=(COLS // TILE,),
        in_specs=[
            pl.BlockSpec(block, own),
            pl.BlockSpec(block, oth),
            pl.BlockSpec(block, own),
            pl.BlockSpec(block, oth),
            pl.BlockSpec((1, RANK, TILE), own3),
            pl.BlockSpec((1, RANK, TILE), oth3),
        ],
        out_specs=[
            pl.BlockSpec((ROWS, TILE), lambda j, s: (0, j)),
            pl.BlockSpec((ROWS, TILE), lambda j, s: (0, j)),
            pl.BlockSpec((RANK, ROWS), lambda j, s: (0, 0)),
            pl.BlockSpec((RANK, ROWS), lambda j, s: (0, 0)),
        ],
    )
    return pl.pallas_call(
        correct_kernel,
        grid_spec=grid_spec,
        out_shape=[
            jax.ShapeDtypeStruct((ROWS, COLS), F32),
            jax.ShapeDtypeStruct((ROWS, COLS), F32),
            jax.ShapeDtypeStruct((RANK, ROWS), F32),
            jax.ShapeDtypeStruct((RANK, ROWS), F32),
        ],
        compiler_params=params(),
        name="correct",
    )(core, grads, grads, errors, errors, q_prev, q_prev)


def right_kernel(parts, c_own, c_got, raw, left):
    total = jnp.sum(parts[...], axis=0)
    left[...] = total
    l_hi, l_lo = split(total)
    s_hi, s_lo = split(c_own[...] + c_got[...])
    both = matmul(jnp.concatenate([l_hi, l_lo], axis=0), s_hi, ((1,), (0,)))
    value = both[:RANK] + both[RANK:] + matmul(l_hi, s_lo, ((1,), (0,)))
    for k in range(RANK):
        raw[k] = value[k : k + 1]


def right(parts, c_own, c_got):
    return pl.pallas_call(
        right_kernel,
        grid=(COLS // TILE,),
        in_specs=[
            pl.BlockSpec((SIZES["z"], RANK, ROWS), lambda j: (0, 0, 0)),
            pl.BlockSpec((ROWS, TILE), lambda j: (0, j)),
            pl.BlockSpec((ROWS, TILE), lambda j: (0, j)),
        ],
        out_specs=[
            pl.BlockSpec((RANK, 1, TILE), lambda j: (0, 0, j)),
            pl.BlockSpec((RANK, ROWS), lambda j: (0, 0)),
        ],
        out_shape=[
            jax.ShapeDtypeStruct((RANK, 1, COLS), F32),
            jax.ShapeDtypeStruct((RANK, ROWS), F32),
        ],
        compiler_params=params(),
        name="right_terms",
    )(parts, c_own, c_got)


def factor_kernel(left_ref, out):
    left = left_ref[...]
    gram = lax.dot_general(
        left, left, (((1,), (1,)), ((), ())), precision=lax.Precision.HIGHEST, preferred_element_type=F32
    )
    row = lax.broadcasted_iota(jnp.int32, (RANK, RANK), 0)
    col = lax.broadcasted_iota(jnp.int32, (RANK, RANK), 1)
    unit = (row == col).astype(F32)
    work = jnp.concatenate([gram, unit], axis=1)
    below = lax.broadcasted_iota(jnp.int32, (RANK, 2 * RANK), 0)
    for j in range(RANK):
        pivot_row = work[j : j + 1, :]
        pivot = work[j : j + 1, j : j + 1]
        scale = lax.rsqrt(pivot)
        scaled = pivot_row * scale
        column = work[:, j : j + 1] * scale
        work = jnp.where(below > j, work - column * scaled, jnp.where(below == j, scaled, work))
    inverse = work[:, RANK:]
    ortho = lax.dot_general(
        inverse, left, (((1,), (0,)), ((), ())), precision=lax.Precision.HIGHEST, preferred_element_type=F32
    )
    out[0] = ortho
    out[1] = jnp.concatenate([inverse, jnp.zeros((RANK, ROWS - RANK), F32)], axis=1)


def factor(left):
    return pl.pallas_call(
        factor_kernel,
        out_shape=jax.ShapeDtypeStruct((2, RANK, ROWS), F32),
        compiler_params=params(),
        cost_estimate=pl.CostEstimate(flops=10_000_000, bytes_accessed=10_000_000, transcendentals=0),
        name="factor",
    )(left)


def finish_kernel(which_ref, raw, factors, c, *refs):
    rebuilt, new_errors, new_q = refs[-3:]
    rows = jnp.concatenate([raw[k] for k in range(RANK)], axis=0)
    r_hi, r_lo = split(rows)
    i_hi, i_lo = split(factors[1][:, :RANK])
    q = matmul(
        jnp.concatenate([i_hi, i_hi, i_lo], axis=1), jnp.concatenate([r_hi, r_lo, r_hi], axis=0), ((1,), (0,))
    ) * (1.0 / (SIZES["z"] * SIZES["x"] * SIZES["core"]))
    new_q[0] = q
    q_hi, q_lo = split(q)
    o_hi, o_lo = split(factors[0])
    approx = matmul(
        jnp.concatenate([o_hi, o_hi, o_lo], axis=0), jnp.concatenate([q_hi, q_lo, q_hi], axis=0), ((0,), (0,))
    )
    rebuilt[0] = approx.astype(BF16)
    new_errors[0, 0] = c[...] - approx


def finish(which, raw, factors, c, held=()):
    grid_spec = pltpu.PrefetchScalarGridSpec(
        num_scalar_prefetch=1,
        grid=(COLS // TILE,),
        in_specs=[
            pl.BlockSpec((RANK, 1, TILE), lambda j, s: (0, 0, j)),
            pl.BlockSpec((2, RANK, ROWS), lambda j, s: (0, 0, 0)),
            pl.BlockSpec((ROWS, TILE), lambda j, s: (0, j)),
        ]
        + [pl.BlockSpec(memory_space=pl.ANY)] * len(held),
        out_specs=[
            pl.BlockSpec((1, ROWS, TILE), lambda j, s: (s[0], 0, j)),
            pl.BlockSpec((1, 1, ROWS, TILE), lambda j, s: (s[0], 0, 0, j)),
            pl.BlockSpec((1, RANK, TILE), lambda j, s: (s[0], 0, j)),
        ],
    )
    return pl.pallas_call(
        finish_kernel,
        grid_spec=grid_spec,
        out_shape=[
            jax.ShapeDtypeStruct((2, ROWS, COLS), BF16),
            jax.ShapeDtypeStruct((2, 1, ROWS, COLS), F32),
            jax.ShapeDtypeStruct((2, RANK, COLS), F32),
        ],
        input_output_aliases={4 + i: i for i in range(len(held))},
        compiler_params=params(),
        cost_estimate=pl.CostEstimate(flops=50_000_000, bytes_accessed=6_000_000, transcendentals=0),
        name="finish_second" if held else "finish_first",
    )(which, raw, factors, c, *held)


def swap(value):
    return lax.ppermute(value, "core", [(0, 1), (1, 0)])


def copies(value, axes):
    count = 1
    for axis in axes:
        count *= SIZES[axis]
    return lax.all_to_all(jnp.broadcast_to(value[None], (count,) + value.shape), axes, 0, 0, tiled=True)


def shards(grads, errors, q_prev):
    core = lax.axis_index("core").astype(jnp.int32)
    c_own, c_oth, left_own, left_oth = correct(core[None], grads, errors, q_prev)
    left = left_own + swap(left_oth)
    c_got = swap(c_oth)
    left = jnp.sum(copies(left, ("x", "tensor")), axis=0)
    parts = copies(left, ("z",))
    raw, left = right(parts, c_own, c_got)
    factors = factor(left)
    factors_got = swap(factors)
    mine = jnp.sum(lax.all_to_all(raw, ("z", "x"), 0, 0, tiled=True), axis=0)
    raw = copies(mine, ("z", "x"))
    raw_got = swap(raw)
    outs = finish(core[None], raw, factors, c_own)
    return tuple(finish(1 - core[None], raw_got, factors_got, c_oth, outs))


def solution(mesh):
    fine = Mesh(mesh.devices.reshape(tuple(SIZES.values())), tuple(SIZES))
    dp = ("z", "x", "core")
    in_specs = (
        P(None, dp, None, "tensor"),
        P(None, dp, None, "tensor"),
        P(None, None, "tensor"),
    )
    out_specs = (P(None, None, "tensor"), P(None, dp, None, "tensor"), P(None, None, "tensor"))
    return jax.shard_map(shards, mesh=fine, in_specs=in_specs, out_specs=out_specs, check_vma=False)
```

```python
import jax
import jax.numpy as jnp
from jax import lax
from jax.experimental import pallas as pl
from jax.experimental.pallas import tpu as pltpu
from jax.sharding import Mesh
from jax.sharding import PartitionSpec as P

F32 = jnp.float32
BF16 = jnp.bfloat16
SIZES = {"z": 8, "x": 4, "core": 2, "tensor": 4}
RANK = 32
ROWS = 128
COLS = 3200
TILE = 640
CHUNKS = COLS // TILE
VMEM_BYTES = 24 * 1024 * 1024


def params():
    return pltpu.CompilerParams(vmem_limit_bytes=VMEM_BYTES)


def split(value):
    high = value.astype(BF16)
    return high, (value - high.astype(F32)).astype(BF16)


def matmul(a, b, dims):
    return lax.dot_general(a, b, (dims, ((), ())), preferred_element_type=F32)


def correct_kernel(core_ref, grads, errors, q_prev, c_own, c_oth, left_own, left_oth, g_buf, q_buf, sems):
    own = core_ref[0]
    copies_in = []
    for slot, (m, c_out) in enumerate(((1 - own, c_oth), (own, c_own))):
        copies_in.append([pltpu.make_async_copy(q_prev.at[m], q_buf.at[slot], sems.at[slot, 2 * CHUNKS])])
        for j in range(CHUNKS):
            cols = pl.ds(j * TILE, TILE)
            copies_in[slot].append(
                (
                    pltpu.make_async_copy(grads.at[m, 0, :, cols], g_buf.at[slot, j], sems.at[slot, j]),
                    pltpu.make_async_copy(errors.at[m, 0, :, cols], c_out.at[:, cols], sems.at[slot, CHUNKS + j]),
                )
            )
    for slot in range(2):
        copies_in[slot][0].start()
        for g_copy, e_copy in copies_in[slot][1:]:
            g_copy.start()
            e_copy.start()
    for slot, (c_out, left) in enumerate(((c_oth, left_oth), (c_own, left_own))):
        copies_in[slot][0].wait()
        total = jnp.zeros((RANK, ROWS), F32)
        for j in range(CHUNKS):
            cols = pl.ds(j * TILE, TILE)
            for copy in copies_in[slot][1 + j]:
                copy.wait()
            c = g_buf[slot, j].astype(F32) + c_out[:, cols]
            c_out[:, cols] = c
            c_hi, c_lo = split(c)
            q_hi, q_lo = split(q_buf[slot, :, cols])
            both = matmul(jnp.concatenate([q_hi, q_lo], axis=0), c_hi, ((1,), (1,)))
            total += both[:RANK] + both[RANK:] + matmul(q_hi, c_lo, ((1,), (1,)))
        left[...] = total


def in_vmem(count):
    return [pl.BlockSpec(memory_space=pltpu.VMEM)] * count


def anywhere(count):
    return [pl.BlockSpec(memory_space=pl.ANY)] * count


SCALAR = pl.BlockSpec(memory_space=pltpu.SMEM)


def correct(core, grads, errors, q_prev):
    return pl.pallas_call(
        correct_kernel,
        in_specs=[SCALAR] + [pl.BlockSpec(memory_space=pltpu.HBM)] * 3,
        out_specs=in_vmem(4),
        out_shape=[
            jax.ShapeDtypeStruct((ROWS, COLS), F32),
            jax.ShapeDtypeStruct((ROWS, COLS), F32),
            jax.ShapeDtypeStruct((RANK, ROWS), F32),
            jax.ShapeDtypeStruct((RANK, ROWS), F32),
        ],
        scratch_shapes=[
            pltpu.VMEM((2, CHUNKS, ROWS, TILE), BF16),
            pltpu.VMEM((2, RANK, COLS), F32),
            pltpu.SemaphoreType.DMA((2, 2 * CHUNKS + 1)),
        ],
        compiler_params=params(),
        cost_estimate=pl.CostEstimate(flops=300_000_000, bytes_accessed=9_000_000, transcendentals=0),
        name="correct",
    )(core, *[pltpu.with_memory_space_constraint(x, pltpu.HBM) for x in (grads, errors, q_prev)])


def right_kernel(parts, c_own, c_got, raw, left):
    total = jnp.sum(parts[...], axis=0)
    left[...] = total
    l_hi, l_lo = split(total)
    l_both = jnp.concatenate([l_hi, l_lo], axis=0)
    for j in range(CHUNKS):
        cols = pl.ds(j * TILE, TILE)
        s_hi, s_lo = split(c_own[:, cols] + c_got[:, cols])
        both = matmul(l_both, s_hi, ((1,), (0,)))
        value = both[:RANK] + both[RANK:] + matmul(l_hi, s_lo, ((1,), (0,)))
        for k in range(RANK):
            raw[k, :, cols] = value[k : k + 1]


def right(parts, c_own, c_got):
    return pl.pallas_call(
        right_kernel,
        in_specs=in_vmem(3),
        out_specs=in_vmem(2),
        out_shape=[
            jax.ShapeDtypeStruct((RANK, 1, COLS), F32),
            jax.ShapeDtypeStruct((RANK, ROWS), F32),
        ],
        compiler_params=params(),
        cost_estimate=pl.CostEstimate(flops=100_000_000, bytes_accessed=4_000_000, transcendentals=0),
        name="right_terms",
    )(parts, c_own, c_got)


def factor_kernel(left_ref, out):
    left = left_ref[...]
    gram = lax.dot_general(
        left, left, (((1,), (1,)), ((), ())), precision=lax.Precision.HIGHEST, preferred_element_type=F32
    )
    row = lax.broadcasted_iota(jnp.int32, (RANK, RANK), 0)
    col = lax.broadcasted_iota(jnp.int32, (RANK, RANK), 1)
    unit = (row == col).astype(F32)
    work = jnp.concatenate([gram, unit], axis=1)
    below = lax.broadcasted_iota(jnp.int32, (RANK, 2 * RANK), 0)
    for j in range(RANK):
        pivot_row = work[j : j + 1, :]
        pivot = work[j : j + 1, j : j + 1]
        scale = lax.rsqrt(pivot)
        scaled = pivot_row * scale
        column = work[:, j : j + 1] * scale
        work = jnp.where(below > j, work - column * scaled, jnp.where(below == j, scaled, work))
    inverse = work[:, RANK:]
    ortho = lax.dot_general(
        inverse, left, (((1,), (0,)), ((), ())), precision=lax.Precision.HIGHEST, preferred_element_type=F32
    )
    out[0] = ortho
    out[1] = jnp.concatenate([inverse, jnp.zeros((RANK, ROWS - RANK), F32)], axis=1)


def factor(left):
    return pl.pallas_call(
        factor_kernel,
        in_specs=in_vmem(1),
        out_specs=in_vmem(1)[0],
        out_shape=jax.ShapeDtypeStruct((2, RANK, ROWS), F32),
        compiler_params=params(),
        cost_estimate=pl.CostEstimate(flops=10_000_000, bytes_accessed=10_000_000, transcendentals=0),
        name="factor",
    )(left)


def finish_kernel(which_ref, raw, factors, c, *refs):
    rebuilt, new_errors, new_q, r_buf, e_buf, q_buf, sems = refs[-7:]
    m = which_ref[0]
    i_hi, i_lo = split(factors[1][:, :RANK])
    i_all = jnp.concatenate([i_hi, i_hi, i_lo], axis=1)
    o_hi, o_lo = split(factors[0])
    o_all = jnp.concatenate([o_hi, o_hi, o_lo], axis=0)
    out = []
    for j in range(CHUNKS):
        cols = pl.ds(j * TILE, TILE)
        rows = jnp.concatenate([raw[k, :, cols] for k in range(RANK)], axis=0)
        r_hi, r_lo = split(rows)
        q = matmul(i_all, jnp.concatenate([r_hi, r_lo, r_hi], axis=0), ((1,), (0,)))
        q = q * (1.0 / (SIZES["z"] * SIZES["x"] * SIZES["core"]))
        q_buf[:, cols] = q
        q_hi, q_lo = split(q)
        approx = matmul(o_all, jnp.concatenate([q_hi, q_lo, q_hi], axis=0), ((0,), (0,)))
        r_buf[:, cols] = approx.astype(BF16)
        e_buf[:, cols] = c[:, cols] - approx
        out.append(pltpu.make_async_copy(q_buf.at[:, cols], new_q.at[m, :, cols], sems.at[3 * j]))
        out.append(pltpu.make_async_copy(r_buf.at[:, cols], rebuilt.at[m, :, cols], sems.at[3 * j + 1]))
        out.append(pltpu.make_async_copy(e_buf.at[:, cols], new_errors.at[m, 0, :, cols], sems.at[3 * j + 2]))
        for copy in out[-3:]:
            copy.start()
    for copy in out:
        copy.wait()


def finish(which, raw, factors, c, held=()):
    return pl.pallas_call(
        finish_kernel,
        in_specs=[SCALAR] + in_vmem(3) + anywhere(len(held)),
        out_specs=[pl.BlockSpec(memory_space=pltpu.HBM)] * 3,
        out_shape=[
            jax.ShapeDtypeStruct((2, ROWS, COLS), BF16),
            jax.ShapeDtypeStruct((2, 1, ROWS, COLS), F32),
            jax.ShapeDtypeStruct((2, RANK, COLS), F32),
        ],
        scratch_shapes=[
            pltpu.VMEM((ROWS, COLS), BF16),
            pltpu.VMEM((ROWS, COLS), F32),
            pltpu.VMEM((RANK, COLS), F32),
            pltpu.SemaphoreType.DMA((3 * CHUNKS,)),
        ],
        input_output_aliases={4 + i: i for i in range(len(held))},
        compiler_params=params(),
        cost_estimate=pl.CostEstimate(flops=50_000_000, bytes_accessed=6_000_000, transcendentals=0),
        name="finish_second" if held else "finish_first",
    )(which, raw, factors, c, *held)


def swap(value):
    return lax.ppermute(value, "core", [(0, 1), (1, 0)])


def copies(value, axes):
    count = 1
    for axis in axes:
        count *= SIZES[axis]
    return lax.all_to_all(jnp.broadcast_to(value[None], (count,) + value.shape), axes, 0, 0, tiled=True)


def shards(grads, errors, q_prev):
    core = lax.axis_index("core").astype(jnp.int32)
    c_own, c_oth, left_own, left_oth = correct(core[None], grads, errors, q_prev)
    left_got = swap(left_oth)
    left_got, c_oth = lax.optimization_barrier((left_got, c_oth))
    left = left_own + left_got
    c_got = swap(c_oth)
    left = jnp.sum(copies(left, ("x", "tensor")), axis=0)
    parts = copies(left, ("z",))
    raw, left = right(parts, c_own, c_got)
    factors = factor(left)
    mine = jnp.sum(lax.all_to_all(raw, ("z", "x"), 0, 0, tiled=True), axis=0)
    mine, factors = lax.optimization_barrier((mine, factors))
    factors_got = swap(factors)
    raw = copies(mine, ("z", "x"))
    raw_got = swap(raw)
    outs = finish(core[None], raw, factors, c_own)
    return tuple(finish(1 - core[None], raw_got, factors_got, c_oth, outs))


def solution(mesh):
    fine = Mesh(mesh.devices.reshape(tuple(SIZES.values())), tuple(SIZES))
    dp = ("z", "x", "core")
    in_specs = (
        P(None, dp, None, "tensor"),
        P(None, dp, None, "tensor"),
        P(None, None, "tensor"),
    )
    out_specs = (P(None, None, "tensor"), P(None, dp, None, "tensor"), P(None, None, "tensor"))
    return jax.shard_map(shards, mesh=fine, in_specs=in_specs, out_specs=out_specs, check_vma=False)
```

```python
import jax
import jax.numpy as jnp
from jax import lax
from jax.experimental import pallas as pl
from jax.experimental.pallas import tpu as pltpu
from jax.sharding import Mesh
from jax.sharding import PartitionSpec as P

F32 = jnp.float32
BF16 = jnp.bfloat16
SIZES = {"z": 8, "x": 4, "core": 2, "tensor": 4}
RANK = 32
ROWS = 128
COLS = 3200
TILE = 640
CHUNKS = COLS // TILE
PIECES = ((0, 1280), (1280, 1920))
VMEM_BYTES = 24 * 1024 * 1024


def params():
    return pltpu.CompilerParams(vmem_limit_bytes=VMEM_BYTES)


def split(value):
    high = value.astype(BF16)
    return high, (value - high.astype(F32)).astype(BF16)


def matmul(a, b, dims):
    return lax.dot_general(a, b, (dims, ((), ())), preferred_element_type=F32)


def correct_kernel(core_ref, grads, errors, q_prev, c_own, c_send, left_own, left_oth, c_oth, g_buf, q_buf, sems):
    own = core_ref[0]
    count = len(PIECES)
    order = ((1 - own, c_oth, left_oth), (own, c_own, left_own))
    arrivals = []
    for slot, (m, c_out, _) in enumerate(order):
        pieces = []
        for j, (first, width) in enumerate(PIECES):
            cols = pl.ds(first, width)
            pieces.append(
                (
                    pltpu.make_async_copy(grads.at[m, 0, :, cols], g_buf.at[slot, :, cols], sems.at[slot, j]),
                    pltpu.make_async_copy(errors.at[m, 0, :, cols], c_out.at[:, cols], sems.at[slot, count + j]),
                )
            )
        q_copy = pltpu.make_async_copy(q_prev.at[m], q_buf.at[slot], sems.at[slot, 2 * count])
        arrivals.append((q_copy, pieces))
    for q_copy, pieces in arrivals:
        for j, (g_copy, e_copy) in enumerate(pieces):
            g_copy.start()
            e_copy.start()
            if j == 0:
                q_copy.start()
    sends = []
    for slot, (_, c_out, left) in enumerate(order):
        q_copy, pieces = arrivals[slot]
        total = jnp.zeros((RANK, ROWS), F32)
        for j, (first, width) in enumerate(PIECES):
            cols = pl.ds(first, width)
            for copy in pieces[j]:
                copy.wait()
            c = g_buf[slot, :, cols].astype(F32) + c_out[:, cols]
            c_out[:, cols] = c
            if slot == 0:
                sends.append(
                    pltpu.make_async_copy(c_out.at[:, cols], c_send.at[:, cols], sems.at[slot, 2 * count + 1 + j])
                )
                sends[-1].start()
            if j == 0:
                q_copy.wait()
            c_hi, c_lo = split(c)
            q_hi, q_lo = split(q_buf[slot, :, cols])
            both = matmul(jnp.concatenate([q_hi, q_lo], axis=0), c_hi, ((1,), (1,)))
            total += both[:RANK] + both[RANK:] + matmul(q_hi, c_lo, ((1,), (1,)))
        left[...] = total
    for copy in sends:
        copy.wait()


def in_vmem(count):
    return [pl.BlockSpec(memory_space=pltpu.VMEM)] * count


def in_hbm(count):
    return [pl.BlockSpec(memory_space=pltpu.HBM)] * count


def anywhere(count):
    return [pl.BlockSpec(memory_space=pl.ANY)] * count


SCALAR = pl.BlockSpec(memory_space=pltpu.SMEM)


def correct(core, grads, errors, q_prev):
    return pl.pallas_call(
        correct_kernel,
        in_specs=[SCALAR] + in_hbm(3),
        out_specs=in_vmem(1) + in_hbm(1) + in_vmem(2),
        out_shape=[
            pltpu.VMEM((ROWS, COLS), F32),
            pltpu.HBM((ROWS, COLS), F32),
            jax.ShapeDtypeStruct((RANK, ROWS), F32),
            jax.ShapeDtypeStruct((RANK, ROWS), F32),
        ],
        scratch_shapes=[
            pltpu.VMEM((ROWS, COLS), F32),
            pltpu.VMEM((2, ROWS, COLS), BF16),
            pltpu.VMEM((2, RANK, COLS), F32),
            pltpu.SemaphoreType.DMA((2, 3 * len(PIECES) + 1)),
        ],
        compiler_params=params(),
        cost_estimate=pl.CostEstimate(flops=300_000_000, bytes_accessed=9_000_000, transcendentals=0),
        name="correct",
    )(core, *[pltpu.with_memory_space_constraint(x, pltpu.HBM) for x in (grads, errors, q_prev)])


def right_kernel(parts, c_own, c_got, raw, left, raw_buf, sems):
    total = jnp.sum(parts[...], axis=0)
    left[...] = total
    l_hi, l_lo = split(total)
    l_both = jnp.concatenate([l_hi, l_lo], axis=0)
    sends = []
    for j, (first, width) in enumerate(PIECES):
        cols = pl.ds(first, width)
        s_hi, s_lo = split(c_own[:, cols] + c_got[:, cols])
        both = matmul(l_both, s_hi, ((1,), (0,)))
        value = both[:RANK] + both[RANK:] + matmul(l_hi, s_lo, ((1,), (0,)))
        for k in range(RANK):
            raw_buf[k, :, cols] = value[k : k + 1]
        sends.append(pltpu.make_async_copy(raw_buf.at[:, :, cols], raw.at[:, :, cols], sems.at[j]))
        sends[-1].start()
    for copy in sends:
        copy.wait()


def right(parts, c_own, c_got):
    return pl.pallas_call(
        right_kernel,
        in_specs=in_vmem(3),
        out_specs=in_hbm(1) + in_vmem(1),
        out_shape=[
            pltpu.HBM((RANK, 1, COLS), F32),
            jax.ShapeDtypeStruct((RANK, ROWS), F32),
        ],
        scratch_shapes=[
            pltpu.VMEM((RANK, 1, COLS), F32),
            pltpu.SemaphoreType.DMA((len(PIECES),)),
        ],
        compiler_params=params(),
        cost_estimate=pl.CostEstimate(flops=100_000_000, bytes_accessed=4_000_000, transcendentals=0),
        name="right_terms",
    )(parts, c_own, c_got)


def factor_kernel(left_ref, out):
    left = left_ref[...]
    gram = lax.dot_general(
        left, left, (((1,), (1,)), ((), ())), precision=lax.Precision.HIGHEST, preferred_element_type=F32
    )
    row = lax.broadcasted_iota(jnp.int32, (RANK, RANK), 0)
    col = lax.broadcasted_iota(jnp.int32, (RANK, RANK), 1)
    unit = (row == col).astype(F32)
    work = jnp.concatenate([gram, unit], axis=1)
    below = lax.broadcasted_iota(jnp.int32, (RANK, 2 * RANK), 0)
    for j in range(RANK):
        pivot_row = work[j : j + 1, :]
        pivot = work[j : j + 1, j : j + 1]
        scale = lax.rsqrt(pivot)
        scaled = pivot_row * scale
        column = work[:, j : j + 1] * scale
        work = jnp.where(below > j, work - column * scaled, jnp.where(below == j, scaled, work))
    inverse = work[:, RANK:]
    ortho = lax.dot_general(
        inverse, left, (((1,), (0,)), ((), ())), precision=lax.Precision.HIGHEST, preferred_element_type=F32
    )
    out[0] = ortho
    out[1] = jnp.concatenate([inverse, jnp.zeros((RANK, ROWS - RANK), F32)], axis=1)


def factor(left):
    return pl.pallas_call(
        factor_kernel,
        in_specs=in_vmem(1),
        out_specs=in_vmem(1)[0],
        out_shape=jax.ShapeDtypeStruct((2, RANK, ROWS), F32),
        compiler_params=params(),
        cost_estimate=pl.CostEstimate(flops=10_000_000, bytes_accessed=10_000_000, transcendentals=0),
        name="factor",
    )(left)


def finish_kernel(which_ref, raw, factors, c, *refs):
    rebuilt, new_errors, new_q, r_buf, e_buf, q_buf, sems = refs[-7:]
    m = which_ref[0]
    i_hi, i_lo = split(factors[1][:, :RANK])
    i_all = jnp.concatenate([i_hi, i_hi, i_lo], axis=1)
    o_hi, o_lo = split(factors[0])
    o_all = jnp.concatenate([o_hi, o_hi, o_lo], axis=0)
    out = []
    for j in range(CHUNKS):
        cols = pl.ds(j * TILE, TILE)
        rows = jnp.concatenate([raw[k, :, cols] for k in range(RANK)], axis=0)
        r_hi, r_lo = split(rows)
        q = matmul(i_all, jnp.concatenate([r_hi, r_lo, r_hi], axis=0), ((1,), (0,)))
        q = q * (1.0 / (SIZES["z"] * SIZES["x"] * SIZES["core"]))
        q_buf[:, cols] = q
        q_hi, q_lo = split(q)
        approx = matmul(o_all, jnp.concatenate([q_hi, q_lo, q_hi], axis=0), ((0,), (0,)))
        r_buf[:, cols] = approx.astype(BF16)
        e_buf[:, cols] = c[:, cols] - approx
        out.append(pltpu.make_async_copy(q_buf.at[:, cols], new_q.at[m, :, cols], sems.at[3 * j]))
        out.append(pltpu.make_async_copy(r_buf.at[:, cols], rebuilt.at[m, :, cols], sems.at[3 * j + 1]))
        out.append(pltpu.make_async_copy(e_buf.at[:, cols], new_errors.at[m, 0, :, cols], sems.at[3 * j + 2]))
        for copy in out[-3:]:
            copy.start()
    for copy in out:
        copy.wait()


def finish(which, raw, factors, c, held=()):
    return pl.pallas_call(
        finish_kernel,
        in_specs=[SCALAR] + in_vmem(3) + anywhere(len(held)),
        out_specs=in_hbm(3),
        out_shape=[
            jax.ShapeDtypeStruct((2, ROWS, COLS), BF16),
            jax.ShapeDtypeStruct((2, 1, ROWS, COLS), F32),
            jax.ShapeDtypeStruct((2, RANK, COLS), F32),
        ],
        scratch_shapes=[
            pltpu.VMEM((ROWS, COLS), BF16),
            pltpu.VMEM((ROWS, COLS), F32),
            pltpu.VMEM((RANK, COLS), F32),
            pltpu.SemaphoreType.DMA((3 * CHUNKS,)),
        ],
        input_output_aliases={4 + i: i for i in range(len(held))},
        compiler_params=params(),
        cost_estimate=pl.CostEstimate(flops=50_000_000, bytes_accessed=6_000_000, transcendentals=0),
        name="finish_second" if held else "finish_first",
    )(which, raw, factors, c, *held)


def swap(value):
    return lax.ppermute(value, "core", [(0, 1), (1, 0)])


def copies(value, axes):
    count = 1
    for axis in axes:
        count *= SIZES[axis]
    return lax.all_to_all(jnp.broadcast_to(value[None], (count,) + value.shape), axes, 0, 0, tiled=True)


def shards(grads, errors, q_prev):
    core = lax.axis_index("core").astype(jnp.int32)
    c_own, c_oth, left_own, left_oth = correct(core[None], grads, errors, q_prev)
    left_got = swap(left_oth)
    left_got, c_oth = lax.optimization_barrier((left_got, c_oth))
    left = left_own + left_got
    c_got = swap(c_oth)
    left = jnp.sum(copies(left, ("x", "tensor")), axis=0)
    parts = copies(left, ("z",))
    raw, left = right(parts, c_own, c_got)
    factors = factor(left)
    factors_got = swap(factors)
    mine = jnp.sum(lax.all_to_all(raw, ("z", "x"), 0, 0, tiled=True), axis=0)
    mine, factors, factors_got = lax.optimization_barrier((mine, factors, factors_got))
    raw = copies(mine, ("z", "x"))
    raw_got = swap(raw)
    outs = finish(core[None], raw, factors, c_own)
    return tuple(finish(1 - core[None], raw_got, factors_got, c_oth, outs))


def solution(mesh):
    fine = Mesh(mesh.devices.reshape(tuple(SIZES.values())), tuple(SIZES))
    dp = ("z", "x", "core")
    in_specs = (
        P(None, dp, None, "tensor"),
        P(None, dp, None, "tensor"),
        P(None, None, "tensor"),
    )
    out_specs = (P(None, None, "tensor"), P(None, dp, None, "tensor"), P(None, None, "tensor"))
    return jax.shard_map(shards, mesh=fine, in_specs=in_specs, out_specs=out_specs, check_vma=False)
```

```python
import jax
import jax.numpy as jnp
from jax import lax
from jax.experimental import pallas as pl
from jax.experimental.pallas import tpu as pltpu
from jax.sharding import Mesh
from jax.sharding import PartitionSpec as P

F32 = jnp.float32
BF16 = jnp.bfloat16
SIZES = {"z": 8, "x": 4, "core": 2, "tensor": 4}
RANK = 32
ROWS = 128
COLS = 3200
PIECES = ((0, 1280), (1280, 1920))
OUT_PIECES = ((0, 640), (640, 1280), (1920, 1280))
VMEM_BYTES = 24 * 1024 * 1024


def params():
    return pltpu.CompilerParams(vmem_limit_bytes=VMEM_BYTES)


def split(value):
    high = value.astype(BF16)
    return high, (value - high.astype(F32)).astype(BF16)


def matmul(a, b, dims):
    return lax.dot_general(a, b, (dims, ((), ())), preferred_element_type=F32)


def correct_kernel(core_ref, grads, errors, q_prev, c_own, c_send, left_own, left_oth, c_oth, g_buf, q_buf, sems):
    own = core_ref[0]
    count = len(PIECES)
    order = ((1 - own, c_oth, left_oth), (own, c_own, left_own))
    arrivals = []
    for slot, (m, c_out, _) in enumerate(order):
        pieces = []
        for j, (first, width) in enumerate(PIECES):
            cols = pl.ds(first, width)
            pieces.append(
                (
                    pltpu.make_async_copy(grads.at[m, 0, :, cols], g_buf.at[slot, :, cols], sems.at[slot, j]),
                    pltpu.make_async_copy(errors.at[m, 0, :, cols], c_out.at[:, cols], sems.at[slot, count + j]),
                )
            )
        q_copy = pltpu.make_async_copy(q_prev.at[m], q_buf.at[slot], sems.at[slot, 2 * count])
        arrivals.append((q_copy, pieces))
    for q_copy, pieces in arrivals:
        for j, (g_copy, e_copy) in enumerate(pieces):
            g_copy.start()
            e_copy.start()
            if j == 0:
                q_copy.start()
    sends = []
    for slot, (_, c_out, left) in enumerate(order):
        q_copy, pieces = arrivals[slot]
        total = jnp.zeros((RANK, ROWS), F32)
        for j, (first, width) in enumerate(PIECES):
            cols = pl.ds(first, width)
            for copy in pieces[j]:
                copy.wait()
            c = g_buf[slot, :, cols].astype(F32) + c_out[:, cols]
            c_out[:, cols] = c
            if slot == 0:
                sends.append(
                    pltpu.make_async_copy(c_out.at[:, cols], c_send.at[:, cols], sems.at[slot, 2 * count + 1 + j])
                )
                sends[-1].start()
            if j == 0:
                q_copy.wait()
            c_hi, c_lo = split(c)
            q_hi, q_lo = split(q_buf[slot, :, cols])
            both = matmul(jnp.concatenate([q_hi, q_lo], axis=0), c_hi, ((1,), (1,)))
            total += both[:RANK] + both[RANK:] + matmul(q_hi, c_lo, ((1,), (1,)))
        left[...] = total
    for copy in sends:
        copy.wait()


def in_vmem(count):
    return [pl.BlockSpec(memory_space=pltpu.VMEM)] * count


def in_hbm(count):
    return [pl.BlockSpec(memory_space=pltpu.HBM)] * count


def anywhere(count):
    return [pl.BlockSpec(memory_space=pl.ANY)] * count


SCALAR = pl.BlockSpec(memory_space=pltpu.SMEM)


def correct(core, grads, errors, q_prev):
    return pl.pallas_call(
        correct_kernel,
        in_specs=[SCALAR] + in_hbm(3),
        out_specs=in_vmem(1) + in_hbm(1) + in_vmem(2),
        out_shape=[
            pltpu.VMEM((ROWS, COLS), F32),
            pltpu.HBM((ROWS, COLS), F32),
            jax.ShapeDtypeStruct((RANK, ROWS), F32),
            jax.ShapeDtypeStruct((RANK, ROWS), F32),
        ],
        scratch_shapes=[
            pltpu.VMEM((ROWS, COLS), F32),
            pltpu.VMEM((2, ROWS, COLS), BF16),
            pltpu.VMEM((2, RANK, COLS), F32),
            pltpu.SemaphoreType.DMA((2, 3 * len(PIECES) + 1)),
        ],
        compiler_params=params(),
        cost_estimate=pl.CostEstimate(flops=300_000_000, bytes_accessed=9_000_000, transcendentals=0),
        name="correct",
    )(core, *[pltpu.with_memory_space_constraint(x, pltpu.HBM) for x in (grads, errors, q_prev)])


def right_kernel(parts, c_own, c_got, raw, left):
    total = jnp.sum(parts[...], axis=0)
    left[...] = total
    l_hi, l_lo = split(total)
    l_both = jnp.concatenate([l_hi, l_lo], axis=0)
    for first, width in PIECES:
        cols = pl.ds(first, width)
        s_hi, s_lo = split(c_own[:, cols] + c_got[:, cols])
        both = matmul(l_both, s_hi, ((1,), (0,)))
        value = both[:RANK] + both[RANK:] + matmul(l_hi, s_lo, ((1,), (0,)))
        for k in range(RANK):
            raw[k, :, cols] = value[k : k + 1]


def right(parts, c_own, c_got):
    return pl.pallas_call(
        right_kernel,
        in_specs=in_vmem(3),
        out_specs=in_vmem(2),
        out_shape=[
            jax.ShapeDtypeStruct((RANK, 1, COLS), F32),
            jax.ShapeDtypeStruct((RANK, ROWS), F32),
        ],
        compiler_params=params(),
        cost_estimate=pl.CostEstimate(flops=100_000_000, bytes_accessed=4_000_000, transcendentals=0),
        name="right_terms",
    )(parts, c_own, c_got)


def factor_kernel(left_ref, out):
    left = left_ref[...]
    gram = lax.dot_general(
        left, left, (((1,), (1,)), ((), ())), precision=lax.Precision.HIGHEST, preferred_element_type=F32
    )
    row = lax.broadcasted_iota(jnp.int32, (RANK, RANK), 0)
    col = lax.broadcasted_iota(jnp.int32, (RANK, RANK), 1)
    unit = (row == col).astype(F32)
    work = jnp.concatenate([gram, unit], axis=1)
    below = lax.broadcasted_iota(jnp.int32, (RANK, 2 * RANK), 0)
    for j in range(RANK):
        pivot_row = work[j : j + 1, :]
        pivot = work[j : j + 1, j : j + 1]
        scale = lax.rsqrt(pivot)
        scaled = pivot_row * scale
        column = work[:, j : j + 1] * scale
        work = jnp.where(below > j, work - column * scaled, jnp.where(below == j, scaled, work))
    inverse = work[:, RANK:]
    ortho = lax.dot_general(
        inverse, left, (((1,), (0,)), ((), ())), precision=lax.Precision.HIGHEST, preferred_element_type=F32
    )
    twice = lax.dot_general(
        inverse, ortho, (((0,), (0,)), ((), ())), precision=lax.Precision.HIGHEST, preferred_element_type=F32
    )
    share = 1.0 / (SIZES["z"] * SIZES["x"] * SIZES["core"])
    out[0] = twice * share
    out[1] = jnp.concatenate([inverse.T * share, jnp.zeros((RANK, ROWS - RANK), F32)], axis=1)


def factor(left):
    return pl.pallas_call(
        factor_kernel,
        in_specs=in_vmem(1),
        out_specs=in_vmem(1)[0],
        out_shape=jax.ShapeDtypeStruct((2, RANK, ROWS), F32),
        compiler_params=params(),
        cost_estimate=pl.CostEstimate(flops=10_000_000, bytes_accessed=10_000_000, transcendentals=0),
        name="factor",
    )(left)


def finish_kernel(which_ref, raw, factors, c, *refs):
    rebuilt, new_errors, new_q, r_buf, e_buf, q_buf, sems = refs[-7:]
    m = which_ref[0]
    f_hi, f_lo = split(jnp.concatenate([factors[0], factors[1][:, :RANK]], axis=1))
    f_all = jnp.concatenate([f_hi, f_hi, f_lo], axis=0)
    out = []
    for j, (first, width) in enumerate(OUT_PIECES):
        cols = pl.ds(first, width)
        rows = jnp.concatenate([raw[k, :, cols] for k in range(RANK)], axis=0)
        r_hi, r_lo = split(rows)
        both = matmul(f_all, jnp.concatenate([r_hi, r_lo, r_hi], axis=0), ((0,), (0,)))
        approx = both[:ROWS]
        e_buf[:, cols] = c[:, cols] - approx
        out.append(pltpu.make_async_copy(e_buf.at[:, cols], new_errors.at[m, 0, :, cols], sems.at[3 * j]))
        out[-1].start()
        r_buf[:, cols] = approx.astype(BF16)
        out.append(pltpu.make_async_copy(r_buf.at[:, cols], rebuilt.at[m, :, cols], sems.at[3 * j + 1]))
        out[-1].start()
        q_buf[:, cols] = both[ROWS:]
        out.append(pltpu.make_async_copy(q_buf.at[:, cols], new_q.at[m, :, cols], sems.at[3 * j + 2]))
        out[-1].start()
    for copy in out:
        copy.wait()


def finish(which, raw, factors, c, held=()):
    return pl.pallas_call(
        finish_kernel,
        in_specs=[SCALAR] + in_vmem(3) + anywhere(len(held)),
        out_specs=in_hbm(3),
        out_shape=[
            jax.ShapeDtypeStruct((2, ROWS, COLS), BF16),
            jax.ShapeDtypeStruct((2, 1, ROWS, COLS), F32),
            jax.ShapeDtypeStruct((2, RANK, COLS), F32),
        ],
        scratch_shapes=[
            pltpu.VMEM((ROWS, COLS), BF16),
            pltpu.VMEM((ROWS, COLS), F32),
            pltpu.VMEM((RANK, COLS), F32),
            pltpu.SemaphoreType.DMA((3 * len(OUT_PIECES),)),
        ],
        input_output_aliases={4 + i: i for i in range(len(held))},
        compiler_params=params(),
        cost_estimate=pl.CostEstimate(flops=50_000_000, bytes_accessed=6_000_000, transcendentals=0),
        name="finish_second" if held else "finish_first",
    )(which, raw, factors, c, *held)


def swap(value):
    return lax.ppermute(value, "core", [(0, 1), (1, 0)])


def copies(value, axes):
    count = 1
    for axis in axes:
        count *= SIZES[axis]
    return lax.all_to_all(jnp.broadcast_to(value[None], (count,) + value.shape), axes, 0, 0, tiled=True)


def shards(grads, errors, q_prev):
    core = lax.axis_index("core").astype(jnp.int32)
    c_own, c_oth, left_own, left_oth = correct(core[None], grads, errors, q_prev)
    left_got = swap(left_oth)
    left_got, c_oth = lax.optimization_barrier((left_got, c_oth))
    left = left_own + left_got
    c_got = swap(c_oth)
    left = jnp.sum(copies(left, ("x", "tensor")), axis=0)
    parts = copies(left, ("z",))
    raw, left = right(parts, c_own, c_got)
    mine = jnp.sum(lax.all_to_all(raw, ("z", "x"), 0, 0, tiled=True), axis=0)
    mine, left = lax.optimization_barrier((mine, left))
    factors = factor(left)
    factors_got = swap(factors)
    raw = copies(mine, ("z", "x"))
    raw, factors, factors_got = lax.optimization_barrier((raw, factors, factors_got))
    raw_got = swap(raw)
    outs = finish(core[None], raw, factors, c_own)
    return tuple(finish(1 - core[None], raw_got, factors_got, c_oth, outs))


def solution(mesh):
    fine = Mesh(mesh.devices.reshape(tuple(SIZES.values())), tuple(SIZES))
    dp = ("z", "x", "core")
    in_specs = (
        P(None, dp, None, "tensor"),
        P(None, dp, None, "tensor"),
        P(None, None, "tensor"),
    )
    out_specs = (P(None, None, "tensor"), P(None, dp, None, "tensor"), P(None, None, "tensor"))
    return jax.shard_map(shards, mesh=fine, in_specs=in_specs, out_specs=out_specs, check_vma=False)
```

```python
import jax
import jax.numpy as jnp
from jax import lax
from jax.experimental import pallas as pl
from jax.experimental.pallas import tpu as pltpu
from jax.sharding import Mesh
from jax.sharding import PartitionSpec as P

F32 = jnp.float32
BF16 = jnp.bfloat16
SIZES = {"z": 8, "x": 4, "core": 2, "tensor": 4}
RANK = 32
ROWS = 128
COLS = 3200
PIECES = ((0, 1280), (1280, 1920))
GROUPS = 4
OUT_PIECES = ((0, 640), (640, 1280), (1920, 1280))
VMEM_BYTES = 24 * 1024 * 1024


def params():
    return pltpu.CompilerParams(vmem_limit_bytes=VMEM_BYTES)


def split(value):
    high = value.astype(BF16)
    return high, (value - high.astype(F32)).astype(BF16)


def matmul(a, b, dims):
    return lax.dot_general(a, b, (dims, ((), ())), preferred_element_type=F32)


def left_terms(c, q):
    c_hi, c_lo = split(c)
    q_hi, q_lo = split(q)
    both = matmul(jnp.concatenate([q_hi, q_lo], axis=0), c_hi, ((1,), (1,)))
    return both[:RANK] + both[RANK:] + matmul(q_hi, c_lo, ((1,), (1,)))


def other_kernel(
    core_ref, grads, errors, q_prev, c_oth, left, g_own, e_own, q_own, g_oth, q_oth, sems, own_sems
):
    own = core_ref[0]
    oth = 1 - own
    count = len(PIECES)
    arrivals = []
    for j, (first, width) in enumerate(PIECES):
        cols = pl.ds(first, width)
        arrivals.append(
            (
                pltpu.make_async_copy(grads.at[oth, 0, :, cols], g_oth.at[:, cols], sems.at[j]),
                pltpu.make_async_copy(errors.at[oth, 0, :, cols], c_oth.at[:, cols], sems.at[count + j]),
            )
        )
    q_copy = pltpu.make_async_copy(q_prev.at[oth], q_oth, sems.at[2 * count])
    keeps = (
        pltpu.make_async_copy(grads.at[own, 0], g_own, own_sems.at[0]),
        pltpu.make_async_copy(errors.at[own, 0], e_own, own_sems.at[1]),
        pltpu.make_async_copy(q_prev.at[own], q_own, own_sems.at[2]),
    )
    for j, pair in enumerate(arrivals):
        for copy in pair:
            copy.start()
        if j == 0:
            q_copy.start()
    for copy in keeps:
        copy.start()
    total = jnp.zeros((RANK, ROWS), F32)
    for j, (first, width) in enumerate(PIECES):
        cols = pl.ds(first, width)
        for copy in arrivals[j]:
            copy.wait()
        c = g_oth[:, cols].astype(F32) + c_oth[:, cols]
        c_oth[:, cols] = c
        if j == 0:
            q_copy.wait()
        total += left_terms(c, q_oth[:, cols])
    left[...] = total
    for copy in keeps:
        copy.wait()


def own_kernel(g, e, q, c_oth, c_out, left, c_send, sem):
    send = pltpu.make_async_copy(c_oth, c_send, sem)
    send.start()
    total = jnp.zeros((RANK, ROWS), F32)
    for first, width in PIECES:
        cols = pl.ds(first, width)
        c = g[:, cols].astype(F32) + e[:, cols]
        c_out[:, cols] = c
        total += left_terms(c, q[:, cols])
    left[...] = total
    send.wait()


def in_vmem(count):
    return [pl.BlockSpec(memory_space=pltpu.VMEM)] * count


def in_hbm(count):
    return [pl.BlockSpec(memory_space=pltpu.HBM)] * count


def anywhere(count):
    return [pl.BlockSpec(memory_space=pl.ANY)] * count


SCALAR = pl.BlockSpec(memory_space=pltpu.SMEM)


def correct_other(core, grads, errors, q_prev):
    return pl.pallas_call(
        other_kernel,
        in_specs=[SCALAR] + in_hbm(3),
        out_specs=in_vmem(5),
        out_shape=[
            pltpu.VMEM((ROWS, COLS), F32),
            pltpu.VMEM((RANK, ROWS), F32),
            pltpu.VMEM((ROWS, COLS), BF16),
            pltpu.VMEM((ROWS, COLS), F32),
            pltpu.VMEM((RANK, COLS), F32),
        ],
        scratch_shapes=[
            pltpu.VMEM((ROWS, COLS), BF16),
            pltpu.VMEM((RANK, COLS), F32),
            pltpu.SemaphoreType.DMA((2 * len(PIECES) + 1,)),
            pltpu.SemaphoreType.DMA((3,)),
        ],
        compiler_params=params(),
        cost_estimate=pl.CostEstimate(flops=150_000_000, bytes_accessed=9_000_000, transcendentals=0),
        name="correct_other",
    )(core, *[pltpu.with_memory_space_constraint(x, pltpu.HBM) for x in (grads, errors, q_prev)])


def correct_own(g, e, q, c_oth):
    return pl.pallas_call(
        own_kernel,
        in_specs=in_vmem(4),
        out_specs=in_vmem(2) + in_hbm(1),
        out_shape=[pltpu.VMEM((ROWS, COLS), F32), pltpu.VMEM((RANK, ROWS), F32), pltpu.HBM((ROWS, COLS), F32)],
        scratch_shapes=[pltpu.SemaphoreType.DMA],
        compiler_params=params(),
        cost_estimate=pl.CostEstimate(flops=150_000_000, bytes_accessed=4_000_000, transcendentals=0),
        name="correct_own",
    )(g, e, q, c_oth)


def right_kernel(parts, c_own, c_got, raw, left):
    total = jnp.sum(parts[...], axis=0)
    left[...] = total
    l_hi, l_lo = split(total)
    l_both = jnp.concatenate([l_hi, l_lo], axis=0)
    for first, width in PIECES:
        cols = pl.ds(first, width)
        s_hi, s_lo = split(c_own[:, cols] + c_got[:, cols])
        both = matmul(l_both, s_hi, ((1,), (0,)))
        value = both[:RANK] + both[RANK:] + matmul(l_hi, s_lo, ((1,), (0,)))
        for k in range(RANK):
            raw[k, :, cols] = value[k : k + 1]


def right(parts, c_own, c_got):
    return pl.pallas_call(
        right_kernel,
        in_specs=in_vmem(3),
        out_specs=in_vmem(2),
        out_shape=[
            jax.ShapeDtypeStruct((RANK, 1, COLS), F32),
            jax.ShapeDtypeStruct((RANK, ROWS), F32),
        ],
        compiler_params=params(),
        cost_estimate=pl.CostEstimate(flops=100_000_000, bytes_accessed=4_000_000, transcendentals=0),
        name="right_terms",
    )(parts, c_own, c_got)


def spread_kernel(parts, out, buf, sems):
    total = jnp.sum(parts[...], axis=0)
    group = RANK // GROUPS
    for k in range(group):
        buf[k] = total
    sends = [pltpu.make_async_copy(buf, out.at[pl.ds(g * group, group)], sems.at[g]) for g in range(GROUPS)]
    for copy in sends:
        copy.start()
    for copy in sends:
        copy.wait()


def spread(parts):
    return pl.pallas_call(
        spread_kernel,
        in_specs=in_vmem(1),
        out_specs=in_hbm(1)[0],
        out_shape=pltpu.HBM((RANK, 1, COLS), F32),
        scratch_shapes=[
            pltpu.VMEM((RANK // GROUPS, 1, COLS), F32),
            pltpu.SemaphoreType.DMA((GROUPS,)),
        ],
        compiler_params=params(),
        cost_estimate=pl.CostEstimate(flops=100_000, bytes_accessed=1_000_000, transcendentals=0),
        name="spread",
    )(parts)


def factor_kernel(left_ref, out):
    left = left_ref[...]
    gram = lax.dot_general(
        left, left, (((1,), (1,)), ((), ())), precision=lax.Precision.HIGHEST, preferred_element_type=F32
    )
    row = lax.broadcasted_iota(jnp.int32, (RANK, RANK), 0)
    col = lax.broadcasted_iota(jnp.int32, (RANK, RANK), 1)
    unit = (row == col).astype(F32)
    work = jnp.concatenate([gram, unit], axis=1)
    below = lax.broadcasted_iota(jnp.int32, (RANK, 2 * RANK), 0)
    for j in range(RANK):
        pivot_row = work[j : j + 1, :]
        pivot = work[j : j + 1, j : j + 1]
        scale = lax.rsqrt(pivot)
        scaled = pivot_row * scale
        column = work[:, j : j + 1] * scale
        work = jnp.where(below > j, work - column * scaled, jnp.where(below == j, scaled, work))
    inverse = work[:, RANK:]
    ortho = lax.dot_general(
        inverse, left, (((1,), (0,)), ((), ())), precision=lax.Precision.HIGHEST, preferred_element_type=F32
    )
    twice = lax.dot_general(
        inverse, ortho, (((0,), (0,)), ((), ())), precision=lax.Precision.HIGHEST, preferred_element_type=F32
    )
    share = 1.0 / (SIZES["z"] * SIZES["x"] * SIZES["core"])
    out[0] = twice * share
    out[1] = jnp.concatenate([inverse.T * share, jnp.zeros((RANK, ROWS - RANK), F32)], axis=1)


def factor(left):
    return pl.pallas_call(
        factor_kernel,
        in_specs=in_vmem(1),
        out_specs=in_vmem(1)[0],
        out_shape=jax.ShapeDtypeStruct((2, RANK, ROWS), F32),
        compiler_params=params(),
        cost_estimate=pl.CostEstimate(flops=10_000_000, bytes_accessed=10_000_000, transcendentals=0),
        name="factor",
    )(left)


def finish_kernel(which_ref, raw, factors, c, *refs):
    rebuilt, new_errors, new_q, r_buf, e_buf, q_buf, sems = refs[-7:]
    m = which_ref[0]
    f_hi, f_lo = split(jnp.concatenate([factors[0], factors[1][:, :RANK]], axis=1))
    f_all = jnp.concatenate([f_hi, f_hi, f_lo], axis=0)
    out = []
    for j, (first, width) in enumerate(OUT_PIECES):
        cols = pl.ds(first, width)
        rows = jnp.concatenate([raw[k, :, cols] for k in range(RANK)], axis=0)
        r_hi, r_lo = split(rows)
        both = matmul(f_all, jnp.concatenate([r_hi, r_lo, r_hi], axis=0), ((0,), (0,)))
        approx = both[:ROWS]
        e_buf[:, cols] = c[:, cols] - approx
        out.append(pltpu.make_async_copy(e_buf.at[:, cols], new_errors.at[m, 0, :, cols], sems.at[3 * j]))
        out[-1].start()
        r_buf[:, cols] = approx.astype(BF16)
        out.append(pltpu.make_async_copy(r_buf.at[:, cols], rebuilt.at[m, :, cols], sems.at[3 * j + 1]))
        out[-1].start()
        q_buf[:, cols] = both[ROWS:]
        out.append(pltpu.make_async_copy(q_buf.at[:, cols], new_q.at[m, :, cols], sems.at[3 * j + 2]))
        out[-1].start()
    for copy in out:
        copy.wait()


def finish(which, raw, factors, c, held=()):
    return pl.pallas_call(
        finish_kernel,
        in_specs=[SCALAR] + in_vmem(3) + anywhere(len(held)),
        out_specs=in_hbm(3),
        out_shape=[
            jax.ShapeDtypeStruct((2, ROWS, COLS), BF16),
            jax.ShapeDtypeStruct((2, 1, ROWS, COLS), F32),
            jax.ShapeDtypeStruct((2, RANK, COLS), F32),
        ],
        scratch_shapes=[
            pltpu.VMEM((ROWS, COLS), BF16),
            pltpu.VMEM((ROWS, COLS), F32),
            pltpu.VMEM((RANK, COLS), F32),
            pltpu.SemaphoreType.DMA((3 * len(OUT_PIECES),)),
        ],
        input_output_aliases={4 + i: i for i in range(len(held))},
        compiler_params=params(),
        cost_estimate=pl.CostEstimate(flops=50_000_000, bytes_accessed=6_000_000, transcendentals=0),
        name="finish_second" if held else "finish_first",
    )(which, raw, factors, c, *held)


def swap(value):
    return lax.ppermute(value, "core", [(0, 1), (1, 0)])


def copies(value, axes):
    count = 1
    for axis in axes:
        count *= SIZES[axis]
    return lax.all_to_all(jnp.broadcast_to(value[None], (count,) + value.shape), axes, 0, 0, tiled=True)


def shards(grads, errors, q_prev):
    core = lax.axis_index("core").astype(jnp.int32)
    c_oth, left_oth, g_own, e_own, q_own = correct_other(core[None], grads, errors, q_prev)
    left_got = swap(left_oth)
    c_own, left_own, c_oth = correct_own(g_own, e_own, q_own, c_oth)
    left_got, c_oth = lax.optimization_barrier((left_got, c_oth))
    left = left_own + left_got
    c_got = swap(c_oth)
    left = jnp.sum(copies(left, ("x", "tensor")), axis=0)
    parts = copies(left, ("z",))
    raw, left = right(parts, c_own, c_got)
    mine = spread(lax.all_to_all(raw, ("z", "x"), 0, 0, tiled=True))
    mine, left = lax.optimization_barrier((mine, left))
    factors = factor(left)
    factors_got = swap(factors)
    raw = lax.all_to_all(mine, ("z", "x"), 0, 0, tiled=True)
    raw, factors, factors_got = lax.optimization_barrier((raw, factors, factors_got))
    raw_got = swap(raw)
    outs = finish(core[None], raw, factors, c_own)
    return tuple(finish(1 - core[None], raw_got, factors_got, c_oth, outs))


def solution(mesh):
    fine = Mesh(mesh.devices.reshape(tuple(SIZES.values())), tuple(SIZES))
    dp = ("z", "x", "core")
    in_specs = (
        P(None, dp, None, "tensor"),
        P(None, dp, None, "tensor"),
        P(None, None, "tensor"),
    )
    out_specs = (P(None, None, "tensor"), P(None, dp, None, "tensor"), P(None, None, "tensor"))
    return jax.shard_map(shards, mesh=fine, in_specs=in_specs, out_specs=out_specs, check_vma=False)
```

```python
import jax
import jax.numpy as jnp
from jax import lax
from jax.experimental import pallas as pl
from jax.experimental.pallas import tpu as pltpu
from jax.sharding import Mesh
from jax.sharding import PartitionSpec as P

F32 = jnp.float32
BF16 = jnp.bfloat16
SIZES = {"z": 8, "x": 4, "core": 2, "tensor": 4}
RANK = 32
ROWS = 128
COLS = 3200
PIECES = ((0, 1280), (1280, 1920))
GROUPS = 4
OUT_PIECES = ((0, 640), (640, 1280), (1920, 1280))
VMEM_BYTES = 24 * 1024 * 1024


def params():
    return pltpu.CompilerParams(vmem_limit_bytes=VMEM_BYTES)


def split(value):
    high = value.astype(BF16)
    return high, (value - high.astype(F32)).astype(BF16)


def matmul(a, b, dims):
    return lax.dot_general(a, b, (dims, ((), ())), preferred_element_type=F32)


def left_terms(c, q):
    c_hi, c_lo = split(c)
    q_hi, q_lo = split(q)
    q_both = jnp.concatenate([q_hi, q_lo], axis=0)
    both = matmul(q_both, c_hi, ((1,), (1,))) + matmul(q_both, c_lo, ((1,), (1,)))
    return both[:RANK] + both[RANK:]


def other_kernel(
    core_ref, grads, errors, q_prev, c_oth, left, g_own, e_own, q_own, g_oth, q_oth, sems, own_sems
):
    own = core_ref[0]
    oth = 1 - own
    count = len(PIECES)
    arrivals = []
    for j, (first, width) in enumerate(PIECES):
        cols = pl.ds(first, width)
        arrivals.append(
            (
                pltpu.make_async_copy(grads.at[oth, 0, :, cols], g_oth.at[:, cols], sems.at[j]),
                pltpu.make_async_copy(errors.at[oth, 0, :, cols], c_oth.at[:, cols], sems.at[count + j]),
            )
        )
    q_copy = pltpu.make_async_copy(q_prev.at[oth], q_oth, sems.at[2 * count])
    keeps = (
        pltpu.make_async_copy(grads.at[own, 0], g_own, own_sems.at[0]),
        pltpu.make_async_copy(errors.at[own, 0], e_own, own_sems.at[1]),
        pltpu.make_async_copy(q_prev.at[own], q_own, own_sems.at[2]),
    )
    for j, pair in enumerate(arrivals):
        for copy in pair:
            copy.start()
        if j == 0:
            q_copy.start()
    for copy in keeps:
        copy.start()
    total = jnp.zeros((RANK, ROWS), F32)
    for j, (first, width) in enumerate(PIECES):
        cols = pl.ds(first, width)
        for copy in arrivals[j]:
            copy.wait()
        c = g_oth[:, cols].astype(F32) + c_oth[:, cols]
        c_oth[:, cols] = c
        if j == 0:
            q_copy.wait()
        total += left_terms(c, q_oth[:, cols])
    left[...] = total
    for copy in keeps:
        copy.wait()


def own_kernel(g, e, q, c_oth, c_out, left, c_send, sem):
    send = pltpu.make_async_copy(c_oth, c_send, sem)
    send.start()
    total = jnp.zeros((RANK, ROWS), F32)
    for first, width in PIECES:
        cols = pl.ds(first, width)
        c = g[:, cols].astype(F32) + e[:, cols]
        c_out[:, cols] = c
        total += left_terms(c, q[:, cols])
    left[...] = total
    send.wait()


def in_vmem(count):
    return [pl.BlockSpec(memory_space=pltpu.VMEM)] * count


def in_hbm(count):
    return [pl.BlockSpec(memory_space=pltpu.HBM)] * count


def anywhere(count):
    return [pl.BlockSpec(memory_space=pl.ANY)] * count


SCALAR = pl.BlockSpec(memory_space=pltpu.SMEM)


def correct_other(core, grads, errors, q_prev):
    return pl.pallas_call(
        other_kernel,
        in_specs=[SCALAR] + in_hbm(3),
        out_specs=in_vmem(5),
        out_shape=[
            pltpu.VMEM((ROWS, COLS), F32),
            pltpu.VMEM((RANK, ROWS), F32),
            pltpu.VMEM((ROWS, COLS), BF16),
            pltpu.VMEM((ROWS, COLS), F32),
            pltpu.VMEM((RANK, COLS), F32),
        ],
        scratch_shapes=[
            pltpu.VMEM((ROWS, COLS), BF16),
            pltpu.VMEM((RANK, COLS), F32),
            pltpu.SemaphoreType.DMA((2 * len(PIECES) + 1,)),
            pltpu.SemaphoreType.DMA((3,)),
        ],
        compiler_params=params(),
        cost_estimate=pl.CostEstimate(flops=150_000_000, bytes_accessed=9_000_000, transcendentals=0),
        name="correct_other",
    )(core, *[pltpu.with_memory_space_constraint(x, pltpu.HBM) for x in (grads, errors, q_prev)])


def correct_own(g, e, q, c_oth):
    return pl.pallas_call(
        own_kernel,
        in_specs=in_vmem(4),
        out_specs=in_vmem(2) + in_hbm(1),
        out_shape=[pltpu.VMEM((ROWS, COLS), F32), pltpu.VMEM((RANK, ROWS), F32), pltpu.HBM((ROWS, COLS), F32)],
        scratch_shapes=[pltpu.SemaphoreType.DMA],
        compiler_params=params(),
        cost_estimate=pl.CostEstimate(flops=150_000_000, bytes_accessed=4_000_000, transcendentals=0),
        name="correct_own",
    )(g, e, q, c_oth)


def right_kernel(parts, c_own, c_got, raw, left):
    total = jnp.sum(parts[...], axis=0)
    left[...] = total
    l_hi, l_lo = split(total)
    l_both = jnp.concatenate([l_hi, l_lo], axis=0)
    l_both = jnp.concatenate([l_both, l_both], axis=1)
    for first, width in PIECES:
        cols = pl.ds(first, width)
        s_hi, s_lo = split(c_own[:, cols] + c_got[:, cols])
        both = matmul(l_both, jnp.concatenate([s_hi, s_lo], axis=0), ((1,), (0,)))
        value = both[:RANK] + both[RANK:]
        for k in range(RANK):
            raw[k, :, cols] = value[k : k + 1]


def right(parts, c_own, c_got):
    return pl.pallas_call(
        right_kernel,
        in_specs=in_vmem(3),
        out_specs=in_vmem(2),
        out_shape=[
            jax.ShapeDtypeStruct((RANK, 1, COLS), F32),
            jax.ShapeDtypeStruct((RANK, ROWS), F32),
        ],
        compiler_params=params(),
        cost_estimate=pl.CostEstimate(flops=100_000_000, bytes_accessed=4_000_000, transcendentals=0),
        name="right_terms",
    )(parts, c_own, c_got)


def spread_kernel(parts, out, buf, sems):
    total = jnp.sum(parts[...], axis=0)
    group = RANK // GROUPS
    for k in range(group):
        buf[k] = total
    sends = [pltpu.make_async_copy(buf, out.at[pl.ds(g * group, group)], sems.at[g]) for g in range(GROUPS)]
    for copy in sends:
        copy.start()
    for copy in sends:
        copy.wait()


def spread(parts):
    return pl.pallas_call(
        spread_kernel,
        in_specs=in_vmem(1),
        out_specs=in_hbm(1)[0],
        out_shape=pltpu.HBM((RANK, 1, COLS), F32),
        scratch_shapes=[
            pltpu.VMEM((RANK // GROUPS, 1, COLS), F32),
            pltpu.SemaphoreType.DMA((GROUPS,)),
        ],
        compiler_params=params(),
        cost_estimate=pl.CostEstimate(flops=100_000, bytes_accessed=1_000_000, transcendentals=0),
        name="spread",
    )(parts)


def factor_kernel(left_ref, out):
    left = left_ref[...]
    gram = lax.dot_general(
        left, left, (((1,), (1,)), ((), ())), precision=lax.Precision.HIGHEST, preferred_element_type=F32
    )
    row = lax.broadcasted_iota(jnp.int32, (RANK, RANK), 0)
    col = lax.broadcasted_iota(jnp.int32, (RANK, RANK), 1)
    unit = (row == col).astype(F32)
    work = jnp.concatenate([gram, unit], axis=1)
    below = lax.broadcasted_iota(jnp.int32, (RANK, 2 * RANK), 0)
    for j in range(RANK):
        pivot_row = work[j : j + 1, :]
        pivot = work[j : j + 1, j : j + 1]
        scale = lax.rsqrt(pivot)
        scaled = pivot_row * scale
        column = work[:, j : j + 1] * scale
        work = jnp.where(below > j, work - column * scaled, jnp.where(below == j, scaled, work))
    inverse = work[:, RANK:]
    ortho = lax.dot_general(
        inverse, left, (((1,), (0,)), ((), ())), precision=lax.Precision.HIGHEST, preferred_element_type=F32
    )
    twice = lax.dot_general(
        inverse, ortho, (((0,), (0,)), ((), ())), precision=lax.Precision.HIGHEST, preferred_element_type=F32
    )
    share = 1.0 / (SIZES["z"] * SIZES["x"] * SIZES["core"])
    out[0] = twice * share
    out[1] = jnp.concatenate([inverse.T * share, jnp.zeros((RANK, ROWS - RANK), F32)], axis=1)


def factor(left):
    return pl.pallas_call(
        factor_kernel,
        in_specs=in_vmem(1),
        out_specs=in_vmem(1)[0],
        out_shape=jax.ShapeDtypeStruct((2, RANK, ROWS), F32),
        compiler_params=params(),
        cost_estimate=pl.CostEstimate(flops=10_000_000, bytes_accessed=10_000_000, transcendentals=0),
        name="factor",
    )(left)


def finish_kernel(which_ref, raw, factors, c, *refs):
    rebuilt, new_errors, new_q, r_buf, e_buf, q_buf, sems = refs[-7:]
    m = which_ref[0]
    f_hi, f_lo = split(jnp.concatenate([factors[0], factors[1][:, :RANK]], axis=1))
    f_all = jnp.concatenate([f_hi, f_hi, f_lo, f_lo], axis=0)
    out = []
    for j, (first, width) in enumerate(OUT_PIECES):
        cols = pl.ds(first, width)
        rows = jnp.concatenate([raw[k, :, cols] for k in range(RANK)], axis=0)
        r_hi, r_lo = split(rows)
        both = matmul(f_all, jnp.concatenate([r_hi, r_lo, r_hi, r_lo], axis=0), ((0,), (0,)))
        approx = both[:ROWS]
        e_buf[:, cols] = c[:, cols] - approx
        out.append(pltpu.make_async_copy(e_buf.at[:, cols], new_errors.at[m, 0, :, cols], sems.at[3 * j]))
        out[-1].start()
        r_buf[:, cols] = approx.astype(BF16)
        out.append(pltpu.make_async_copy(r_buf.at[:, cols], rebuilt.at[m, :, cols], sems.at[3 * j + 1]))
        out[-1].start()
        q_buf[:, cols] = both[ROWS:]
        out.append(pltpu.make_async_copy(q_buf.at[:, cols], new_q.at[m, :, cols], sems.at[3 * j + 2]))
        out[-1].start()
    for copy in out:
        copy.wait()


def finish(which, raw, factors, c, held=()):
    return pl.pallas_call(
        finish_kernel,
        in_specs=[SCALAR] + in_vmem(3) + anywhere(len(held)),
        out_specs=in_hbm(3),
        out_shape=[
            jax.ShapeDtypeStruct((2, ROWS, COLS), BF16),
            jax.ShapeDtypeStruct((2, 1, ROWS, COLS), F32),
            jax.ShapeDtypeStruct((2, RANK, COLS), F32),
        ],
        scratch_shapes=[
            pltpu.VMEM((ROWS, COLS), BF16),
            pltpu.VMEM((ROWS, COLS), F32),
            pltpu.VMEM((RANK, COLS), F32),
            pltpu.SemaphoreType.DMA((3 * len(OUT_PIECES),)),
        ],
        input_output_aliases={4 + i: i for i in range(len(held))},
        compiler_params=params(),
        cost_estimate=pl.CostEstimate(flops=50_000_000, bytes_accessed=6_000_000, transcendentals=0),
        name="finish_second" if held else "finish_first",
    )(which, raw, factors, c, *held)


def swap(value):
    return lax.ppermute(value, "core", [(0, 1), (1, 0)])


def copies(value, axes):
    count = 1
    for axis in axes:
        count *= SIZES[axis]
    return lax.all_to_all(jnp.broadcast_to(value[None], (count,) + value.shape), axes, 0, 0, tiled=True)


def shards(grads, errors, q_prev):
    core = lax.axis_index("core").astype(jnp.int32)
    c_oth, left_oth, g_own, e_own, q_own = correct_other(core[None], grads, errors, q_prev)
    left_got = swap(left_oth)
    c_own, left_own, c_oth = correct_own(g_own, e_own, q_own, c_oth)
    left_got, c_oth = lax.optimization_barrier((left_got, c_oth))
    left = left_own + left_got
    c_got = swap(c_oth)
    left = jnp.sum(copies(left, ("x", "tensor")), axis=0)
    parts = copies(left, ("z",))
    raw, left = right(parts, c_own, c_got)
    mine = spread(lax.all_to_all(raw, ("z", "x"), 0, 0, tiled=True))
    mine, left = lax.optimization_barrier((mine, left))
    factors = factor(left)
    factors_got = swap(factors)
    raw = lax.all_to_all(mine, ("z", "x"), 0, 0, tiled=True)
    raw, factors, factors_got = lax.optimization_barrier((raw, factors, factors_got))
    raw_got = swap(raw)
    outs = finish(core[None], raw, factors, c_own)
    return tuple(finish(1 - core[None], raw_got, factors_got, c_oth, outs))


def solution(mesh):
    fine = Mesh(mesh.devices.reshape(tuple(SIZES.values())), tuple(SIZES))
    dp = ("z", "x", "core")
    in_specs = (
        P(None, dp, None, "tensor"),
        P(None, dp, None, "tensor"),
        P(None, None, "tensor"),
    )
    out_specs = (P(None, None, "tensor"), P(None, dp, None, "tensor"), P(None, None, "tensor"))
    return jax.shard_map(shards, mesh=fine, in_specs=in_specs, out_specs=out_specs, check_vma=False)
```

```python
import jax
import jax.numpy as jnp
from jax import lax
from jax.experimental import pallas as pl
from jax.experimental.pallas import tpu as pltpu
from jax.sharding import Mesh
from jax.sharding import PartitionSpec as P

F32 = jnp.float32
BF16 = jnp.bfloat16
SIZES = {"z": 8, "x": 4, "core": 2, "tensor": 4}
RANK = 32
ROWS = 128
COLS = 3200
PIECES = ((0, 1280), (1280, 1920))
IN_PIECES = ((0, 1024), (1024, 1024), (2048, 768), (2816, 384))
GROUPS = 4
OUT_PIECES = ((0, 640), (640, 1280), (1920, 1280))
VMEM_BYTES = 24 * 1024 * 1024


def params():
    return pltpu.CompilerParams(vmem_limit_bytes=VMEM_BYTES)


def split(value):
    high = value.astype(BF16)
    return high, (value - high.astype(F32)).astype(BF16)


def matmul(a, b, dims):
    return lax.dot_general(a, b, (dims, ((), ())), preferred_element_type=F32)


def left_terms(c, q):
    c_hi, c_lo = split(c)
    q_hi, q_lo = split(q)
    q_both = jnp.concatenate([q_hi, q_lo], axis=0)
    both = matmul(q_both, c_hi, ((1,), (1,))) + matmul(q_both, c_lo, ((1,), (1,)))
    return both[:RANK] + both[RANK:]


def other_kernel(
    core_ref, grads, errors, q_prev, c_oth, left, g_own, e_own, q_own, g_oth, q_oth, sems, own_sems
):
    own = core_ref[0]
    oth = 1 - own
    count = len(IN_PIECES)
    arrivals = []
    for j, (first, width) in enumerate(IN_PIECES):
        cols = pl.ds(first, width)
        arrivals.append(
            (
                pltpu.make_async_copy(grads.at[oth, 0, :, cols], g_oth.at[:, cols], sems.at[j]),
                pltpu.make_async_copy(errors.at[oth, 0, :, cols], c_oth.at[:, cols], sems.at[count + j]),
            )
        )
    q_copy = pltpu.make_async_copy(q_prev.at[oth], q_oth, sems.at[2 * count])
    keeps = (
        pltpu.make_async_copy(grads.at[own, 0], g_own, own_sems.at[0]),
        pltpu.make_async_copy(errors.at[own, 0], e_own, own_sems.at[1]),
        pltpu.make_async_copy(q_prev.at[own], q_own, own_sems.at[2]),
    )
    for j, pair in enumerate(arrivals):
        for copy in pair:
            copy.start()
        if j == 0:
            q_copy.start()
    for copy in keeps:
        copy.start()
    total = jnp.zeros((RANK, ROWS), F32)
    for j, (first, width) in enumerate(IN_PIECES):
        cols = pl.ds(first, width)
        for copy in arrivals[j]:
            copy.wait()
        c = g_oth[:, cols].astype(F32) + c_oth[:, cols]
        c_oth[:, cols] = c
        if j == 0:
            q_copy.wait()
        total += left_terms(c, q_oth[:, cols])
    left[...] = total
    for copy in keeps:
        copy.wait()


def own_kernel(g, e, q, c_oth, c_out, left, c_send, sem):
    send = pltpu.make_async_copy(c_oth, c_send, sem)
    send.start()
    total = jnp.zeros((RANK, ROWS), F32)
    for first, width in PIECES:
        cols = pl.ds(first, width)
        c = g[:, cols].astype(F32) + e[:, cols]
        c_out[:, cols] = c
        total += left_terms(c, q[:, cols])
    left[...] = total
    send.wait()


def in_vmem(count):
    return [pl.BlockSpec(memory_space=pltpu.VMEM)] * count


def in_hbm(count):
    return [pl.BlockSpec(memory_space=pltpu.HBM)] * count


def anywhere(count):
    return [pl.BlockSpec(memory_space=pl.ANY)] * count


SCALAR = pl.BlockSpec(memory_space=pltpu.SMEM)


def correct_other(core, grads, errors, q_prev):
    return pl.pallas_call(
        other_kernel,
        in_specs=[SCALAR] + in_hbm(3),
        out_specs=in_vmem(5),
        out_shape=[
            pltpu.VMEM((ROWS, COLS), F32),
            pltpu.VMEM((RANK, ROWS), F32),
            pltpu.VMEM((ROWS, COLS), BF16),
            pltpu.VMEM((ROWS, COLS), F32),
            pltpu.VMEM((RANK, COLS), F32),
        ],
        scratch_shapes=[
            pltpu.VMEM((ROWS, COLS), BF16),
            pltpu.VMEM((RANK, COLS), F32),
            pltpu.SemaphoreType.DMA((2 * len(IN_PIECES) + 1,)),
            pltpu.SemaphoreType.DMA((3,)),
        ],
        compiler_params=params(),
        cost_estimate=pl.CostEstimate(flops=150_000_000, bytes_accessed=9_000_000, transcendentals=0),
        name="correct_other",
    )(core, *[pltpu.with_memory_space_constraint(x, pltpu.HBM) for x in (grads, errors, q_prev)])


def correct_own(g, e, q, c_oth):
    return pl.pallas_call(
        own_kernel,
        in_specs=in_vmem(4),
        out_specs=in_vmem(2) + in_hbm(1),
        out_shape=[pltpu.VMEM((ROWS, COLS), F32), pltpu.VMEM((RANK, ROWS), F32), pltpu.HBM((ROWS, COLS), F32)],
        scratch_shapes=[pltpu.SemaphoreType.DMA],
        compiler_params=params(),
        cost_estimate=pl.CostEstimate(flops=150_000_000, bytes_accessed=4_000_000, transcendentals=0),
        name="correct_own",
    )(g, e, q, c_oth)


def right_kernel(parts, c_own, c_got, raw, left):
    total = jnp.sum(parts[...], axis=0)
    left[...] = total
    l_hi, l_lo = split(total)
    l_both = jnp.concatenate([l_hi, l_lo], axis=0)
    l_both = jnp.concatenate([l_both, l_both], axis=1)
    for first, width in PIECES:
        cols = pl.ds(first, width)
        s_hi, s_lo = split(c_own[:, cols] + c_got[:, cols])
        both = matmul(l_both, jnp.concatenate([s_hi, s_lo], axis=0), ((1,), (0,)))
        value = both[:RANK] + both[RANK:]
        for k in range(RANK):
            raw[k, :, cols] = value[k : k + 1]


def right(parts, c_own, c_got):
    return pl.pallas_call(
        right_kernel,
        in_specs=in_vmem(3),
        out_specs=in_vmem(2),
        out_shape=[
            jax.ShapeDtypeStruct((RANK, 1, COLS), F32),
            jax.ShapeDtypeStruct((RANK, ROWS), F32),
        ],
        compiler_params=params(),
        cost_estimate=pl.CostEstimate(flops=100_000_000, bytes_accessed=4_000_000, transcendentals=0),
        name="right_terms",
    )(parts, c_own, c_got)


def spread_kernel(parts, out, buf, sems):
    total = jnp.sum(parts[...], axis=0)
    group = RANK // GROUPS
    for k in range(group):
        buf[k] = total
    sends = [pltpu.make_async_copy(buf, out.at[pl.ds(g * group, group)], sems.at[g]) for g in range(GROUPS)]
    for copy in sends:
        copy.start()
    for copy in sends:
        copy.wait()


def spread(parts):
    return pl.pallas_call(
        spread_kernel,
        in_specs=in_vmem(1),
        out_specs=in_hbm(1)[0],
        out_shape=pltpu.HBM((RANK, 1, COLS), F32),
        scratch_shapes=[
            pltpu.VMEM((RANK // GROUPS, 1, COLS), F32),
            pltpu.SemaphoreType.DMA((GROUPS,)),
        ],
        compiler_params=params(),
        cost_estimate=pl.CostEstimate(flops=100_000, bytes_accessed=1_000_000, transcendentals=0),
        name="spread",
    )(parts)


def factor_kernel(left_ref, out):
    left = left_ref[...]
    gram = lax.dot_general(
        left, left, (((1,), (1,)), ((), ())), precision=lax.Precision.HIGHEST, preferred_element_type=F32
    )
    row = lax.broadcasted_iota(jnp.int32, (RANK, RANK), 0)
    col = lax.broadcasted_iota(jnp.int32, (RANK, RANK), 1)
    unit = (row == col).astype(F32)
    work = jnp.concatenate([gram, unit], axis=1)
    below = lax.broadcasted_iota(jnp.int32, (RANK, 2 * RANK), 0)
    for j in range(RANK):
        pivot_row = work[j : j + 1, :]
        pivot = work[j : j + 1, j : j + 1]
        scale = lax.rsqrt(pivot)
        scaled = pivot_row * scale
        column = work[:, j : j + 1] * scale
        work = jnp.where(below > j, work - column * scaled, jnp.where(below == j, scaled, work))
    inverse = work[:, RANK:]
    ortho = lax.dot_general(
        inverse, left, (((1,), (0,)), ((), ())), precision=lax.Precision.HIGHEST, preferred_element_type=F32
    )
    twice = lax.dot_general(
        inverse, ortho, (((0,), (0,)), ((), ())), precision=lax.Precision.HIGHEST, preferred_element_type=F32
    )
    share = 1.0 / (SIZES["z"] * SIZES["x"] * SIZES["core"])
    out[0] = twice * share
    out[1] = jnp.concatenate([inverse.T * share, jnp.zeros((RANK, ROWS - RANK), F32)], axis=1)


def factor(left):
    return pl.pallas_call(
        factor_kernel,
        in_specs=in_vmem(1),
        out_specs=in_vmem(1)[0],
        out_shape=jax.ShapeDtypeStruct((2, RANK, ROWS), F32),
        compiler_params=params(),
        cost_estimate=pl.CostEstimate(flops=10_000_000, bytes_accessed=10_000_000, transcendentals=0),
        name="factor",
    )(left)


def finish_kernel(which_ref, raw, factors, c, *refs):
    rebuilt, new_errors, new_q, r_buf, e_buf, q_buf, sems = refs[-7:]
    m = which_ref[0]
    f_hi, f_lo = split(jnp.concatenate([factors[0], factors[1][:, :RANK]], axis=1))
    f_all = jnp.concatenate([f_hi, f_hi, f_lo, f_lo], axis=0)
    out = []
    for j, (first, width) in enumerate(OUT_PIECES):
        cols = pl.ds(first, width)
        rows = jnp.concatenate([raw[k, :, cols] for k in range(RANK)], axis=0)
        r_hi, r_lo = split(rows)
        both = matmul(f_all, jnp.concatenate([r_hi, r_lo, r_hi, r_lo], axis=0), ((0,), (0,)))
        approx = both[:ROWS]
        e_buf[:, cols] = c[:, cols] - approx
        out.append(pltpu.make_async_copy(e_buf.at[:, cols], new_errors.at[m, 0, :, cols], sems.at[3 * j]))
        out[-1].start()
        r_buf[:, cols] = approx.astype(BF16)
        out.append(pltpu.make_async_copy(r_buf.at[:, cols], rebuilt.at[m, :, cols], sems.at[3 * j + 1]))
        out[-1].start()
        q_buf[:, cols] = both[ROWS:]
        out.append(pltpu.make_async_copy(q_buf.at[:, cols], new_q.at[m, :, cols], sems.at[3 * j + 2]))
        out[-1].start()
    for copy in out:
        copy.wait()


def finish(which, raw, factors, c, held=()):
    return pl.pallas_call(
        finish_kernel,
        in_specs=[SCALAR] + in_vmem(3) + anywhere(len(held)),
        out_specs=in_hbm(3),
        out_shape=[
            jax.ShapeDtypeStruct((2, ROWS, COLS), BF16),
            jax.ShapeDtypeStruct((2, 1, ROWS, COLS), F32),
            jax.ShapeDtypeStruct((2, RANK, COLS), F32),
        ],
        scratch_shapes=[
            pltpu.VMEM((ROWS, COLS), BF16),
            pltpu.VMEM((ROWS, COLS), F32),
            pltpu.VMEM((RANK, COLS), F32),
            pltpu.SemaphoreType.DMA((3 * len(OUT_PIECES),)),
        ],
        input_output_aliases={4 + i: i for i in range(len(held))},
        compiler_params=params(),
        cost_estimate=pl.CostEstimate(flops=50_000_000, bytes_accessed=6_000_000, transcendentals=0),
        name="finish_second" if held else "finish_first",
    )(which, raw, factors, c, *held)


def swap(value):
    return lax.ppermute(value, "core", [(0, 1), (1, 0)])


def copies(value, axes):
    count = 1
    for axis in axes:
        count *= SIZES[axis]
    return lax.all_to_all(jnp.broadcast_to(value[None], (count,) + value.shape), axes, 0, 0, tiled=True)


def shards(grads, errors, q_prev):
    core = lax.axis_index("core").astype(jnp.int32)
    c_oth, left_oth, g_own, e_own, q_own = correct_other(core[None], grads, errors, q_prev)
    left_got = swap(left_oth)
    c_own, left_own, c_oth = correct_own(g_own, e_own, q_own, c_oth)
    left_got, c_oth = lax.optimization_barrier((left_got, c_oth))
    left = left_own + left_got
    c_got = swap(c_oth)
    left = jnp.sum(copies(left, ("x", "tensor")), axis=0)
    parts = copies(left, ("z",))
    raw, left = right(parts, c_own, c_got)
    mine = spread(lax.all_to_all(raw, ("z", "x"), 0, 0, tiled=True))
    mine, left = lax.optimization_barrier((mine, left))
    factors = factor(left)
    factors_got = swap(factors)
    raw = lax.all_to_all(mine, ("z", "x"), 0, 0, tiled=True)
    raw, factors, factors_got = lax.optimization_barrier((raw, factors, factors_got))
    raw_got = swap(raw)
    outs = finish(core[None], raw, factors, c_own)
    return tuple(finish(1 - core[None], raw_got, factors_got, c_oth, outs))


def solution(mesh):
    fine = Mesh(mesh.devices.reshape(tuple(SIZES.values())), tuple(SIZES))
    dp = ("z", "x", "core")
    in_specs = (
        P(None, dp, None, "tensor"),
        P(None, dp, None, "tensor"),
        P(None, None, "tensor"),
    )
    out_specs = (P(None, None, "tensor"), P(None, dp, None, "tensor"), P(None, None, "tensor"))
    return jax.shard_map(shards, mesh=fine, in_specs=in_specs, out_specs=out_specs, check_vma=False)
```

```python
import jax
import jax.numpy as jnp
from jax import lax
from jax.experimental import pallas as pl
from jax.experimental.pallas import tpu as pltpu
from jax.sharding import Mesh
from jax.sharding import PartitionSpec as P

F32 = jnp.float32
BF16 = jnp.bfloat16
SIZES = {"z": 8, "x": 4, "core": 2, "tensor": 4}
RANK = 32
ROWS = 128
COLS = 3200
PIECES = ((0, 1280), (1280, 1920))
IN_PIECES = ((0, 1024), (1024, 1024), (2048, 768), (2816, 384))
GROUPS = 4
OUT_PIECES = ((0, 896), (896, 896), (1792, 896), (2688, 512))
VMEM_BYTES = 24 * 1024 * 1024


def params():
    return pltpu.CompilerParams(vmem_limit_bytes=VMEM_BYTES)


def split(value):
    high = value.astype(BF16)
    return high, (value - high.astype(F32)).astype(BF16)


def matmul(a, b, dims):
    return lax.dot_general(a, b, (dims, ((), ())), preferred_element_type=F32)


def left_terms(c, q):
    c_hi, c_lo = split(c)
    q_hi, q_lo = split(q)
    q_both = jnp.concatenate([q_hi, q_lo], axis=0)
    both = matmul(q_both, c_hi, ((1,), (1,))) + matmul(q_both, c_lo, ((1,), (1,)))
    return both[:RANK] + both[RANK:]


def other_kernel(
    core_ref, grads, errors, q_prev, c_oth, left, g_own, e_own, q_own, g_oth, q_oth, sems, own_sems
):
    own = core_ref[0]
    oth = 1 - own
    count = len(IN_PIECES)
    arrivals = []
    for j, (first, width) in enumerate(IN_PIECES):
        cols = pl.ds(first, width)
        arrivals.append(
            (
                pltpu.make_async_copy(grads.at[oth, 0, :, cols], g_oth.at[:, cols], sems.at[j]),
                pltpu.make_async_copy(errors.at[oth, 0, :, cols], c_oth.at[:, cols], sems.at[count + j]),
            )
        )
    q_copy = pltpu.make_async_copy(q_prev.at[oth], q_oth, sems.at[2 * count])
    keeps = (
        pltpu.make_async_copy(grads.at[own, 0], g_own, own_sems.at[0]),
        pltpu.make_async_copy(errors.at[own, 0], e_own, own_sems.at[1]),
        pltpu.make_async_copy(q_prev.at[own], q_own, own_sems.at[2]),
    )
    for j, pair in enumerate(arrivals):
        for copy in pair:
            copy.start()
        if j == 0:
            q_copy.start()
    for copy in keeps:
        copy.start()
    total = jnp.zeros((RANK, ROWS), F32)
    for j, (first, width) in enumerate(IN_PIECES):
        cols = pl.ds(first, width)
        for copy in arrivals[j]:
            copy.wait()
        c = g_oth[:, cols].astype(F32) + c_oth[:, cols]
        c_oth[:, cols] = c
        if j == 0:
            q_copy.wait()
        total += left_terms(c, q_oth[:, cols])
    left[...] = total
    for copy in keeps:
        copy.wait()


def own_kernel(g, e, q, c_oth, c_out, left, c_send, sem):
    send = pltpu.make_async_copy(c_oth, c_send, sem)
    send.start()
    total = jnp.zeros((RANK, ROWS), F32)
    for first, width in PIECES:
        cols = pl.ds(first, width)
        c = g[:, cols].astype(F32) + e[:, cols]
        c_out[:, cols] = c
        total += left_terms(c, q[:, cols])
    left[...] = total
    send.wait()


def in_vmem(count):
    return [pl.BlockSpec(memory_space=pltpu.VMEM)] * count


def in_hbm(count):
    return [pl.BlockSpec(memory_space=pltpu.HBM)] * count


def anywhere(count):
    return [pl.BlockSpec(memory_space=pl.ANY)] * count


SCALAR = pl.BlockSpec(memory_space=pltpu.SMEM)


def correct_other(core, grads, errors, q_prev):
    return pl.pallas_call(
        other_kernel,
        in_specs=[SCALAR] + in_hbm(3),
        out_specs=in_vmem(5),
        out_shape=[
            pltpu.VMEM((ROWS, COLS), F32),
            pltpu.VMEM((RANK, ROWS), F32),
            pltpu.VMEM((ROWS, COLS), BF16),
            pltpu.VMEM((ROWS, COLS), F32),
            pltpu.VMEM((RANK, COLS), F32),
        ],
        scratch_shapes=[
            pltpu.VMEM((ROWS, COLS), BF16),
            pltpu.VMEM((RANK, COLS), F32),
            pltpu.SemaphoreType.DMA((2 * len(IN_PIECES) + 1,)),
            pltpu.SemaphoreType.DMA((3,)),
        ],
        compiler_params=params(),
        cost_estimate=pl.CostEstimate(flops=150_000_000, bytes_accessed=9_000_000, transcendentals=0),
        name="correct_other",
    )(core, *[pltpu.with_memory_space_constraint(x, pltpu.HBM) for x in (grads, errors, q_prev)])


def correct_own(g, e, q, c_oth):
    return pl.pallas_call(
        own_kernel,
        in_specs=in_vmem(4),
        out_specs=in_vmem(2) + in_hbm(1),
        out_shape=[pltpu.VMEM((ROWS, COLS), F32), pltpu.VMEM((RANK, ROWS), F32), pltpu.HBM((ROWS, COLS), F32)],
        scratch_shapes=[pltpu.SemaphoreType.DMA],
        compiler_params=params(),
        cost_estimate=pl.CostEstimate(flops=150_000_000, bytes_accessed=4_000_000, transcendentals=0),
        name="correct_own",
    )(g, e, q, c_oth)


def right_kernel(parts, c_own, c_got, raw, left):
    total = jnp.sum(parts[...], axis=0)
    left[...] = total
    l_hi, l_lo = split(total)
    l_both = jnp.concatenate([l_hi, l_lo], axis=0)
    l_both = jnp.concatenate([l_both, l_both], axis=1)
    for first, width in PIECES:
        cols = pl.ds(first, width)
        s_hi, s_lo = split(c_own[:, cols] + c_got[:, cols])
        both = matmul(l_both, jnp.concatenate([s_hi, s_lo], axis=0), ((1,), (0,)))
        value = both[:RANK] + both[RANK:]
        for k in range(RANK):
            raw[k, :, cols] = value[k : k + 1]


def right(parts, c_own, c_got):
    return pl.pallas_call(
        right_kernel,
        in_specs=in_vmem(3),
        out_specs=in_vmem(2),
        out_shape=[
            jax.ShapeDtypeStruct((RANK, 1, COLS), F32),
            jax.ShapeDtypeStruct((RANK, ROWS), F32),
        ],
        compiler_params=params(),
        cost_estimate=pl.CostEstimate(flops=100_000_000, bytes_accessed=4_000_000, transcendentals=0),
        name="right_terms",
    )(parts, c_own, c_got)


def spread_kernel(parts, out, buf, sems):
    total = jnp.sum(parts[...], axis=0)
    group = RANK // GROUPS
    for k in range(group):
        buf[k] = total
    sends = [pltpu.make_async_copy(buf, out.at[pl.ds(g * group, group)], sems.at[g]) for g in range(GROUPS)]
    for copy in sends:
        copy.start()
    for copy in sends:
        copy.wait()


def spread(parts):
    return pl.pallas_call(
        spread_kernel,
        in_specs=in_vmem(1),
        out_specs=in_hbm(1)[0],
        out_shape=pltpu.HBM((RANK, 1, COLS), F32),
        scratch_shapes=[
            pltpu.VMEM((RANK // GROUPS, 1, COLS), F32),
            pltpu.SemaphoreType.DMA((GROUPS,)),
        ],
        compiler_params=params(),
        cost_estimate=pl.CostEstimate(flops=100_000, bytes_accessed=1_000_000, transcendentals=0),
        name="spread",
    )(parts)


def factor_kernel(left_ref, out):
    left = left_ref[...]
    gram = lax.dot_general(
        left, left, (((1,), (1,)), ((), ())), precision=lax.Precision.HIGHEST, preferred_element_type=F32
    )
    row = lax.broadcasted_iota(jnp.int32, (RANK, RANK), 0)
    col = lax.broadcasted_iota(jnp.int32, (RANK, RANK), 1)
    unit = (row == col).astype(F32)
    work = jnp.concatenate([gram, unit], axis=1)
    below = lax.broadcasted_iota(jnp.int32, (RANK, 2 * RANK), 0)
    for j in range(RANK):
        pivot_row = work[j : j + 1, :]
        pivot = work[j : j + 1, j : j + 1]
        scale = lax.rsqrt(pivot)
        scaled = pivot_row * scale
        column = work[:, j : j + 1] * scale
        work = jnp.where(below > j, work - column * scaled, jnp.where(below == j, scaled, work))
    inverse = work[:, RANK:]
    ortho = lax.dot_general(
        inverse, left, (((1,), (0,)), ((), ())), precision=lax.Precision.HIGHEST, preferred_element_type=F32
    )
    twice = lax.dot_general(
        inverse, ortho, (((0,), (0,)), ((), ())), precision=lax.Precision.HIGHEST, preferred_element_type=F32
    )
    share = 1.0 / (SIZES["z"] * SIZES["x"] * SIZES["core"])
    out[0] = twice * share
    out[1] = jnp.concatenate([inverse.T * share, jnp.zeros((RANK, ROWS - RANK), F32)], axis=1)


def factor(left):
    return pl.pallas_call(
        factor_kernel,
        in_specs=in_vmem(1),
        out_specs=in_vmem(1)[0],
        out_shape=jax.ShapeDtypeStruct((2, RANK, ROWS), F32),
        compiler_params=params(),
        cost_estimate=pl.CostEstimate(flops=10_000_000, bytes_accessed=10_000_000, transcendentals=0),
        name="factor",
    )(left)


def finish_kernel(which_ref, raw, factors, c, *refs):
    rebuilt, new_errors, new_q, r_buf, e_buf, q_buf, sems = refs[-7:]
    m = which_ref[0]
    f_hi, f_lo = split(jnp.concatenate([factors[0], factors[1][:, :RANK]], axis=1))
    f_all = jnp.concatenate([f_hi, f_hi, f_lo, f_lo], axis=0)
    out = []
    for j, (first, width) in enumerate(OUT_PIECES):
        cols = pl.ds(first, width)
        rows = jnp.concatenate([raw[k, :, cols] for k in range(RANK)], axis=0)
        r_hi, r_lo = split(rows)
        both = matmul(f_all, jnp.concatenate([r_hi, r_lo, r_hi, r_lo], axis=0), ((0,), (0,)))
        approx = both[:ROWS]
        e_buf[:, cols] = c[:, cols] - approx
        out.append(pltpu.make_async_copy(e_buf.at[:, cols], new_errors.at[m, 0, :, cols], sems.at[3 * j]))
        out[-1].start()
        r_buf[:, cols] = approx.astype(BF16)
        out.append(pltpu.make_async_copy(r_buf.at[:, cols], rebuilt.at[m, :, cols], sems.at[3 * j + 1]))
        out[-1].start()
        q_buf[:, cols] = both[ROWS:]
        out.append(pltpu.make_async_copy(q_buf.at[:, cols], new_q.at[m, :, cols], sems.at[3 * j + 2]))
        out[-1].start()
    for copy in out:
        copy.wait()


def finish(which, raw, factors, c, held=()):
    return pl.pallas_call(
        finish_kernel,
        in_specs=[SCALAR] + in_vmem(3) + anywhere(len(held)),
        out_specs=in_hbm(3),
        out_shape=[
            jax.ShapeDtypeStruct((2, ROWS, COLS), BF16),
            jax.ShapeDtypeStruct((2, 1, ROWS, COLS), F32),
            jax.ShapeDtypeStruct((2, RANK, COLS), F32),
        ],
        scratch_shapes=[
            pltpu.VMEM((ROWS, COLS), BF16),
            pltpu.VMEM((ROWS, COLS), F32),
            pltpu.VMEM((RANK, COLS), F32),
            pltpu.SemaphoreType.DMA((3 * len(OUT_PIECES),)),
        ],
        input_output_aliases={4 + i: i for i in range(len(held))},
        compiler_params=params(),
        cost_estimate=pl.CostEstimate(flops=50_000_000, bytes_accessed=6_000_000, transcendentals=0),
        name="finish_second" if held else "finish_first",
    )(which, raw, factors, c, *held)


def swap(value):
    return lax.ppermute(value, "core", [(0, 1), (1, 0)])


def copies(value, axes):
    count = 1
    for axis in axes:
        count *= SIZES[axis]
    return lax.all_to_all(jnp.broadcast_to(value[None], (count,) + value.shape), axes, 0, 0, tiled=True)


def shards(grads, errors, q_prev):
    core = lax.axis_index("core").astype(jnp.int32)
    c_oth, left_oth, g_own, e_own, q_own = correct_other(core[None], grads, errors, q_prev)
    left_got = swap(left_oth)
    c_own, left_own, c_oth = correct_own(g_own, e_own, q_own, c_oth)
    left_got, c_oth = lax.optimization_barrier((left_got, c_oth))
    left = left_own + left_got
    c_got = swap(c_oth)
    left = jnp.sum(copies(left, ("x", "tensor")), axis=0)
    parts = copies(left, ("z",))
    raw, left = right(parts, c_own, c_got)
    mine = spread(lax.all_to_all(raw, ("z", "x"), 0, 0, tiled=True))
    mine, left = lax.optimization_barrier((mine, left))
    factors = factor(left)
    factors_got = swap(factors)
    raw = lax.all_to_all(mine, ("z", "x"), 0, 0, tiled=True)
    raw, factors, factors_got = lax.optimization_barrier((raw, factors, factors_got))
    raw_got = swap(raw)
    outs = finish(core[None], raw, factors, c_own)
    return tuple(finish(1 - core[None], raw_got, factors_got, c_oth, outs))


def solution(mesh):
    fine = Mesh(mesh.devices.reshape(tuple(SIZES.values())), tuple(SIZES))
    dp = ("z", "x", "core")
    in_specs = (
        P(None, dp, None, "tensor"),
        P(None, dp, None, "tensor"),
        P(None, None, "tensor"),
    )
    out_specs = (P(None, None, "tensor"), P(None, dp, None, "tensor"), P(None, None, "tensor"))
    return jax.shard_map(shards, mesh=fine, in_specs=in_specs, out_specs=out_specs, check_vma=False)
```
